32 devices in a mesh: space: 4 (over y, core), ctx: 8 (over z, x).
Axes of the slice: x: 2, y: 2, z: 4, core: 2. Of those that a mesh axis runs over, the one named last changes fastest.
Arguments:
- feats: bfloat16 [4, 8192, 256], P('space', 'ctx'), may hold values from -6 to 6
- face_rows: int32 [4, 2048], P('space', 'ctx'), may hold values from 0 to 1023
- neighbours: int32 [4, 8192, 6], P('space', 'ctx'), may hold values from 0 to 2048
- block_len: int32 [4, 64], P('space'), may hold values from 32 to 128
- dilated: int32 [4, 64, 4], P('space', 'ctx'), may hold values from 0 to 7, as said below
- pick: int32 [4, 8, 8], P('space'), may hold values from 0 to 7
- cpe_weight: bfloat16 [7, 256, 256], replicated, may hold values from -0.125 to 0.125
- cpe_bias: float32 [256], replicated, may hold values from -3 to 3
- ln_gain: float32 [256], replicated, may hold values from 0.1 to 1.9
- ln_bias: float32 [256], replicated, may hold values from -3 to 3
- w_qkv: bfloat16 [256, 768], replicated, may hold values from -11 to 11
- w_out: bfloat16 [256, 256], replicated, may hold values from -3 to 3
Outputs:
- mixed: bfloat16 [4, 8192, 256], P('space', 'ctx')
The draws below stay inside these ranges and needn't reach their ends.
Inputs may be any that keep to these rules, and one draw needn't show every extreme that they name: `dilated`: among the 32 entries of the blocks of one range, every value 0 to 7 appears.
All inputs are finite; a program needn't handle non-finite values.
Results may differ from the reference program's by a relative error of at most 0.009.
The reference program's roundings to bfloat16 on the way count: a program that leaves them out, or rounds other values in their place, can miss the bound.
Values may be sent and summed in bfloat16 or wider, within the bound.
A program may use at most 128 MiB of HBM per device.

```python
import math
import jax
import jax.numpy as jnp
from jax import lax

D = 256
HEADS = 8
BLK = 128
DILATED_BLOCKS = 4
EDGE = 128
FACE = 256
VOX_DEV = 1024
SCENE_TILES = 4
SEQ = 8192
RANGE_BLOCKS = 8
TILE_BLOCKS = 64
N_SPACE = 4
N_CTX = 8


def draw_neighbours(key, part):
    keys_all = jax.random.split(key, 6)
    draw_shape = (SCENE_TILES, SEQ, 6)
    block_category = jax.random.randint(keys_all[0], draw_shape, 0, 20)
    lower_edge = jax.random.randint(keys_all[1], draw_shape, 0, EDGE)
    upper_edge = jax.random.randint(keys_all[2], draw_shape, EDGE + VOX_DEV, 2 * EDGE + VOX_DEV)
    face_start = VOX_DEV + 2 * EDGE
    lower_face = jax.random.randint(keys_all[3], draw_shape, face_start, face_start + FACE)
    upper_face = jax.random.randint(keys_all[4], draw_shape, face_start + 2 * FACE, face_start + 3 * FACE)
    own_rows = jax.random.randint(keys_all[5], draw_shape, EDGE, EDGE + VOX_DEV)
    missing = face_start + 3 * FACE
    selected_keys = jnp.where(block_category < 11, upper_face, own_rows)
    selected_keys = jnp.where(block_category < 9, lower_face, selected_keys)
    selected_keys = jnp.where(block_category < 7, upper_edge, selected_keys)
    selected_keys = jnp.where(block_category < 5, lower_edge, selected_keys)
    selected_keys = jnp.where(block_category < 3, missing, selected_keys)
    return selected_keys.astype(jnp.int32)


def draw_block_len(key, part):
    keys_all = jax.random.split(key, 3)
    lengths = jax.random.randint(keys_all[0], (SCENE_TILES, TILE_BLOCKS), BLK // 4, BLK + 1)
    first_col = jax.random.randint(keys_all[1], (SCENE_TILES,), 0, TILE_BLOCKS)
    second_col = (first_col + 1 + jax.random.randint(keys_all[2], (SCENE_TILES,), 0, TILE_BLOCKS - 1)) % TILE_BLOCKS
    tile_ids = jnp.arange(SCENE_TILES)
    lengths = lengths.at[tile_ids, first_col].set(BLK)
    lengths = lengths.at[tile_ids, second_col].set(BLK // 4)
    return lengths.astype(jnp.int32)


def draw_dilated(key, part):
    subkeys = jax.random.split(key, SCENE_TILES * N_CTX)
    orders = jax.vmap(lambda subkey: jax.random.permutation(subkey, N_CTX))(subkeys).astype(jnp.int32)
    memory_reads = jnp.arange(RANGE_BLOCKS * DILATED_BLOCKS) % N_CTX
    selected_keys = orders[:, memory_reads]
    return selected_keys.reshape(SCENE_TILES, TILE_BLOCKS, DILATED_BLOCKS).astype(jnp.int32)


def draw_w_qkv(key, part):
    keys_all = jax.random.split(key, 3)
    norm_scale = D ** (-0.5)
    w_key = jnp.clip(jax.random.normal(keys_all[0], (D, D), jnp.float32), -4.0, 4.0) * norm_scale
    w_value = jnp.clip(jax.random.normal(keys_all[1], (D, D), jnp.float32), -4.0, 4.0) * norm_scale
    noise = jnp.clip(jax.random.normal(keys_all[2], (D, D), jnp.float32), -4.0, 4.0) * norm_scale
    w_query = noise
    return jnp.concatenate([w_query, w_key, w_value], 1).astype(jnp.bfloat16)


def with_ends(result, stream_key, low, high):
    longest = result.shape.index(max(result.shape))
    spots = []
    for shift in (0, 1):
        where = [jax.random.randint(jax.random.fold_in(stream_key, axis), (), 0, length) for axis, length in enumerate(result.shape)]
        where[longest] = (where[longest] + shift) % result.shape[longest]
        spots.append(tuple(where))
    return result.at[spots[0]].set(low).at[spots[1]].set(high)


def block_levels(own_key, extent, pieces, low, high):
    level, own = 1.0, jax.random.fold_in(own_key, 6)
    for axis_at, parts in pieces:
        draws = jnp.exp(jax.random.uniform(jax.random.fold_in(own, axis_at), (parts,), jnp.float32, low / len(pieces), high / len(pieces)))
        level = level * jnp.repeat(draws, extent[axis_at] // parts).reshape([-1 if axis == axis_at else 1 for axis in range(len(extent))])
    return level


def normal_values(key, extent, width, limit, shards=(), kind=jnp.bfloat16):
    factor_of = block_levels(key, extent, shards, -0.22, 0.18) if shards else 1.0
    entries = jax.random.normal(key, extent, jnp.float32) * width * factor_of
    return jnp.minimum(jnp.maximum(entries, -limit), limit).astype(kind)


def setup_inputs(seed: int = 0) -> dict:
    splits = jax.random.split(jax.random.key(seed), 13)
    feats = normal_values(splits[0], (SCENE_TILES, SEQ, D), 1.0, 6.0, ((0, 4), (1, 8)))
    face_rows = with_ends(jax.random.randint(splits[1], (SCENE_TILES, N_CTX * FACE), 0, VOX_DEV), jax.random.fold_in(splits[1], 1), 0, VOX_DEV - 1).astype(jnp.int32)
    neighbours = draw_neighbours(jax.random.fold_in(splits[12], 71), 0)
    block_len = draw_block_len(jax.random.fold_in(splits[12], 71), 0)
    dilated = draw_dilated(jax.random.fold_in(splits[12], 71), 0)
    pick = with_ends(jax.random.randint(splits[5], (SCENE_TILES, N_CTX, N_CTX), 0, RANGE_BLOCKS), jax.random.fold_in(splits[5], 1), 0, RANGE_BLOCKS - 1).astype(jnp.int32)
    cpe_weight = normal_values(splits[6], (7, D, D), (7 * D) ** -0.5, 0.125)
    cpe_bias = normal_values(splits[7], (D,), 0.5, 3.0, (), jnp.float32)
    ln_gain = jnp.clip(1.0 + 0.18 * jax.random.normal(splits[8], (D,), jnp.float32), 0.1, 1.9)
    ln_bias = normal_values(splits[9], (D,), 0.5, 3.0, (), jnp.float32)
    w_qkv = draw_w_qkv(jax.random.fold_in(splits[12], 71), 0)
    w_out = normal_values(splits[11], (D, D), (max(D // 64, 1)) ** -0.5, 3.0)
    return dict(feats=feats, face_rows=face_rows, neighbours=neighbours, block_len=block_len, dilated=dilated, pick=pick, cpe_weight=cpe_weight, cpe_bias=cpe_bias, ln_gain=ln_gain, ln_bias=ln_bias, w_qkv=w_qkv, w_out=w_out)


def layer_norm(hidden, ln_gain, ln_bias):
    center = hidden - lax.optimization_barrier(jnp.mean(hidden, axis=-1, keepdims=True))
    variance = lax.optimization_barrier(jnp.mean(center * center, axis=-1, keepdims=True))
    return (center * lax.rsqrt(variance + 1e-05) * ln_gain + ln_bias).astype(jnp.bfloat16)

def attend(query_blk, key_rows, value_rows, valid_keys):
    rows_q = query_blk.shape[0]
    head_dim = D // HEADS
    query_heads = query_blk.astype(jnp.float32).reshape(rows_q, HEADS, head_dim)
    key_heads = key_rows.astype(jnp.float32).reshape(-1, HEADS, head_dim)
    value_heads = value_rows.astype(jnp.float32).reshape(-1, HEADS, head_dim)
    scores = jnp.einsum('qhd,khd->hqk', query_heads, key_heads) * (1.0 / math.sqrt(head_dim))
    scores = jnp.where(valid_keys[None, None, :], scores, -1e+30)
    row_peak = lax.optimization_barrier(jnp.max(scores, axis=-1, keepdims=True))
    raw_weights = jnp.exp(scores - row_peak)
    denominator = lax.optimization_barrier(jnp.sum(raw_weights, axis=-1, keepdims=True))
    attn_weights = (raw_weights / denominator).astype(jnp.bfloat16)
    mixed_heads = jnp.einsum('hqk,khd->qhd', attn_weights.astype(jnp.float32), value_heads)
    return mixed_heads.reshape(rows_q, D).astype(jnp.bfloat16)

def as_index(value):
    return jnp.asarray(value).astype(jnp.int32)

def reference(feats, face_rows, neighbours, block_len, dilated, pick, cpe_weight, cpe_bias, ln_gain, ln_bias, w_qkv, w_out):
    seq_len = VOX_DEV * N_CTX
    zero_index = as_index(0)
    per_range = feats.reshape(N_SPACE, N_CTX, VOX_DEV, D)
    face_ids = face_rows.reshape(N_SPACE, N_CTX, FACE)
    faces = jax.vmap(jax.vmap(lambda rows_all, picked: rows_all[picked]))(per_range, face_ids)
    empty_face = jnp.zeros((1, N_CTX, FACE, D), feats.dtype)
    faces_pad = jnp.concatenate([empty_face, faces, empty_face], 0)
    feats_pad = jnp.pad(feats, ((0, 0), (EDGE, EDGE), (0, 0)))

    def encode(index):
        tile = as_index(index // N_CTX)
        range_id = as_index(index % N_CTX)
        row_start = as_index(range_id * VOX_DEV)
        edge_rows = lax.dynamic_slice(feats_pad, (tile, row_start, zero_index), (1, VOX_DEV + 2 * EDGE, D))[0]
        face_block = lax.dynamic_slice(faces_pad, (tile, range_id, zero_index, zero_index), (3, 1, FACE, D)).reshape(3 * FACE, D)
        neighbour_table = jnp.concatenate([edge_rows, face_block, jnp.zeros((1, D), feats.dtype)], 0)
        table_ids = lax.dynamic_slice(neighbours, (tile, row_start, zero_index), (1, VOX_DEV, 6))[0]
        own_rows = edge_rows[EDGE:EDGE + VOX_DEV]
        conv_out = jnp.dot(own_rows, cpe_weight[0], preferred_element_type=jnp.float32)
        for offset in range(6):
            conv_out = conv_out + jnp.dot(neighbour_table[table_ids[:, offset]], cpe_weight[offset + 1], preferred_element_type=jnp.float32)
        hidden = own_rows.astype(jnp.float32) + conv_out + cpe_bias
        normed = layer_norm(hidden, ln_gain, ln_bias)
        projected = jnp.dot(normed, w_qkv, preferred_element_type=jnp.float32)
        return (hidden, projected[:, :D].astype(jnp.bfloat16), projected[:, D:2 * D].astype(jnp.bfloat16), projected[:, 2 * D:].astype(jnp.bfloat16))
    hidden, queries, keys_all, values_all = lax.map(encode, jnp.arange(N_SPACE * N_CTX, dtype=jnp.int32))
    hidden = hidden.reshape(N_SPACE, seq_len, D)
    queries = queries.reshape(N_SPACE, seq_len, D)
    keys_all = keys_all.reshape(N_SPACE, seq_len, D)
    values_all = values_all.reshape(N_SPACE, seq_len, D)
    blocks_dev = VOX_DEV // BLK
    blocks_tile = blocks_dev * N_CTX
    keys_pad = jnp.pad(keys_all, ((0, 0), (BLK, BLK), (0, 0)))
    values_pad = jnp.pad(values_all, ((0, 0), (BLK, BLK), (0, 0)))
    lens_ext = jnp.pad(block_len, ((0, 0), (1, 1)))
    positions = jnp.arange(BLK, dtype=jnp.int32)

    def attend_block(index):
        tile = as_index(index // blocks_tile)
        block = as_index(index % blocks_tile)
        range_id = as_index(block // blocks_dev)
        row_start = as_index(block * BLK)
        query_blk = lax.dynamic_slice(queries, (tile, row_start, zero_index), (1, BLK, D))[0]
        window_keys = lax.dynamic_slice(keys_pad, (tile, row_start, zero_index), (1, 3 * BLK, D))[0]
        window_values = lax.dynamic_slice(values_pad, (tile, row_start, zero_index), (1, 3 * BLK, D))[0]
        win_lens = lax.dynamic_slice(lens_ext, (tile, block), (1, 3))[0]
        slot_ids = dilated[tile, block]
        far_ids = as_index(slot_ids * blocks_dev + pick[tile, slot_ids, range_id])
        row_ids = as_index((far_ids[:, None] * BLK + positions[None, :]).reshape(-1))
        remote_keys = keys_all[tile, row_ids]
        remote_values = values_all[tile, row_ids]
        far_lens = block_len[tile, far_ids]
        lens_row = jnp.concatenate([win_lens, far_lens], 0)
        valid_keys = (positions[None, :] < lens_row[:, None]).reshape(-1)
        attended = attend(query_blk, jnp.concatenate([window_keys, remote_keys], 0), jnp.concatenate([window_values, remote_values], 0), valid_keys)
        hidden_block = lax.dynamic_slice(hidden, (tile, row_start, zero_index), (1, BLK, D))[0]
        return (hidden_block + jnp.dot(attended, w_out, preferred_element_type=jnp.float32)).astype(jnp.bfloat16)
    output = lax.map(attend_block, jnp.arange(N_SPACE * blocks_tile, dtype=jnp.int32))
    return output.reshape(N_SPACE, seq_len, D)
```

```python
import functools
import math

import jax
import jax.numpy as jnp
from jax import lax
from jax.experimental import pallas as pl
from jax.experimental.pallas import tpu as pltpu
from jax.sharding import PartitionSpec as P

D = 256
HEADS = 8
BLK = 128
EDGE = 128
FACE = 256
HALF = 128
OFFSETS = 6

MESH = pl.DeviceIdType.MESH
BF16 = jnp.bfloat16
F32 = jnp.float32

LOCAL_PARTS = tuple(range(1, 9)) + (12, 13)
SENT_PARTS = (0, 9, 10, 11, 14, 15)
EARLY = 4


def zero_like(value):
    return jnp.zeros_like(value)


def body(
    n_space, n_ctx,
    feats, face_rows, neighbours, block_len, dilated, pick, cpe_weight, cpe_bias, ln_gain, ln_bias, w_qkv, w_out,
    out_ref,
    table, rows_v, ids_v, weight_v, bias_v, gain_v, shift_v, qkv_v, outw_v,
    lens_s, slots_s, pick_s, pos_s, perm_s,
    early, hidden_s, query_s, normed_s, key_s, value_s, ones_s, outgoing, ends, far,
    near_peak, near_sum, near_den,
    load_sem, table_send, table_recv, send_sem, recv_sem,
):
    space, ctx = lax.axis_index("space"), lax.axis_index("ctx")
    blocks = feats.shape[0]
    count = blocks * BLK
    local = count + FACE

    barrier = pltpu.get_barrier_semaphore()

    def ctx_peer(j):
        half = n_ctx // 2
        mine = ctx // half
        other = (1 - mine) * half + lax.rem(ctx + j, half)
        same = mine * half + lax.rem(ctx + j + 1, half)
        return jnp.where(j < half, other, same)

    for j in range(n_ctx - 1):
        pl.semaphore_signal(barrier, inc=1, device_id=(space, ctx_peer(j)), device_id_type=MESH)
    sides = (
        (ctx < n_ctx - 1, ctx > 0, (space, ctx + 1)),
        (ctx > 0, ctx < n_ctx - 1, (space, ctx - 1)),
        (space < n_space - 1, space > 0, (space + 1, ctx)),
        (space > 0, space < n_space - 1, (space - 1, ctx)),
    )
    for there, _, peer in sides[2:]:
        @pl.when(there)
        def _():
            pl.semaphore_signal(barrier, inc=1, device_id=peer, device_id_type=MESH)

    loads = [
        pltpu.make_async_copy(source, target, load_sem.at[i])
        for i, (source, target) in enumerate((
            (feats, table.at[pl.ds(0, blocks)]),
            (face_rows, rows_v),
            (pick, pick_s),
            (neighbours, ids_v),
            (block_len, lens_s),
            (dilated, slots_s),
            (cpe_weight, weight_v),
            (cpe_bias, bias_v),
            (ln_gain, gain_v),
            (ln_bias, shift_v),
            (w_qkv, qkv_v),
            (w_out, outw_v),
        ))
    ]
    for load in loads:
        load.start()

    lane = lax.broadcasted_iota(jnp.int32, (BLK, HALF), 1)
    row = lax.broadcasted_iota(jnp.int32, (BLK, 1), 0)

    def split_ids(columns):
        spread = jnp.concatenate([jnp.broadcast_to(ids, (BLK, BLK)).T for ids in columns], 0)
        lanes = lax.broadcasted_iota(jnp.int32, spread.shape, 1)
        hot = jnp.where((spread & (BLK - 1)) == lanes, 1.0, 0.0).astype(BF16)
        return hot, (spread >> 7).astype(F32).astype(BF16)

    def choose(hot, high, parts):
        return jnp.concatenate([jnp.where(high == BF16(part), hot, zero_like(hot)) for part in parts], 1)

    loads[0].wait()
    loads[1].wait()
    hot, high = split_ids([rows_v[:, i * BLK : (i + 1) * BLK] for i in range(FACE // BLK)])
    table[blocks : local // BLK] = jnp.dot(
        choose(hot, high, range(blocks)), table[:blocks].reshape(count, D), preferred_element_type=F32
    ).astype(BF16).reshape(FACE // BLK, BLK, D)

    pl.semaphore_wait(
        barrier, n_ctx - 1 + sides[2][0].astype(jnp.int32) + sides[3][0].astype(jnp.int32)
    )
    pieces = (
        (count - EDGE, local, EDGE),
        (0, local + EDGE, EDGE),
        (count, local + 2 * EDGE, FACE),
        (count, local + 2 * EDGE + FACE, FACE),
    )
    copies = [
        pltpu.make_async_remote_copy(
            src_ref=table.at[pl.ds(source // BLK, size // BLK)],
            dst_ref=table.at[pl.ds(target // BLK, size // BLK)],
            send_sem=table_send.at[i],
            recv_sem=table_recv.at[i],
            device_id=sides[i][2],
            device_id_type=MESH,
        )
        for i, (source, target, size) in enumerate(pieces)
    ]
    for i in (2, 3, 0, 1):
        pl.when(sides[i][0])(copies[i].start)
    for i, (_, target, size) in enumerate(pieces):
        @pl.when(jnp.logical_not(sides[i][1]))
        def _():
            table[target // BLK : (target + size) // BLK] = jnp.zeros((size // BLK, BLK, D), BF16)

    loads[2].wait()
    wanted = [pick_s[0, ctx, ctx_peer(j)] for j in range(n_ctx)]
    need = [jnp.int32(n_ctx + b) for b in range(blocks)]
    for j in reversed(range(n_ctx)):
        need = [jnp.where(wanted[j] == b, j, need[b]) for b in range(blocks)]
    position = [
        sum((need[a] < need[b]).astype(jnp.int32) for a in range(blocks) if a != b) for b in range(blocks)
    ]
    for b in range(blocks):
        pos_s[b] = position[b]
    for j in range(blocks):
        perm_s[j] = sum(jnp.where(position[b] == j, b, 0) for b in range(blocks))

    for load in loads[3:]:
        load.wait()

    def block_at(ref, index):
        return ref[index]

    def table_rows(first, last):
        return table[first // BLK : last // BLK].reshape(last - first, D)

    def step_ids(j):
        at = perm_s[j]
        return split_ids([ids_v[o, at] for o in range(OFFSETS)])

    def pick_early(j, carry):
        hot, high = step_ids(j)
        early[j] = jnp.dot(
            choose(hot, high, LOCAL_PARTS), table_rows(0, local), preferred_element_type=F32
        ).astype(BF16)
        return carry

    lax.fori_loop(0, EARLY, pick_early, 0)

    for i in range(4):
        pl.when(sides[i][0])(copies[i].wait_send)
        pl.when(sides[i][1])(copies[i].wait_recv)

    def keep(index, keys, values, valid, spare):
        inside = row < valid
        key_s[index] = jnp.where(inside, keys, spare).astype(BF16)
        value_s[index] = jnp.where(inside, values, 0.0).astype(BF16)
        ones_s[index] = jnp.where(jnp.broadcast_to(inside, (BLK, HALF)), 1.0, 0.0).astype(BF16)

    def send(j):
        return pltpu.make_async_remote_copy(
            src_ref=outgoing.at[j],
            dst_ref=far.at[ctx],
            send_sem=send_sem.at[j],
            recv_sem=recv_sem.at[j],
            device_id=(space, ctx_peer(j)),
            device_id_type=MESH,
        )

    def start_send(j):
        outgoing[j] = block_at(normed_s, pos_s[pick_s[0, ctx, ctx_peer(j)]])
        send(j).start()

    def finish(j, picked):
        block = perm_s[j]
        own = block_at(table, block)
        taps = jnp.concatenate([own] + [picked[o * BLK : (o + 1) * BLK] for o in range(OFFSETS)], 1)
        conv = jnp.dot(taps, weight_v[...], preferred_element_type=F32)
        hidden = own.astype(F32) + conv + bias_v[...]
        hidden_s[j] = hidden
        center = hidden - jnp.mean(hidden, axis=-1, keepdims=True)
        variance = jnp.mean(center * center, axis=-1, keepdims=True)
        normed = (center * lax.rsqrt(variance + 1e-05) * gain_v[...] + shift_v[...]).astype(BF16)
        normed_s[j] = normed
        projected = jnp.dot(normed, qkv_v[...], preferred_element_type=F32)
        query_s[j] = projected[:, :D].astype(BF16)
        keys = projected[:, D : 2 * D]
        keep(j, keys, projected[:, 2 * D :], lens_s[0, ctx * blocks + block], keys[:1])

        @pl.when(j < n_ctx - 1)
        def _():
            start_send(j)

    def finish_early(j, carry):
        hot, high = step_ids(j)
        sent = jnp.dot(choose(hot, high, SENT_PARTS), table_rows(local, table.shape[0] * BLK), preferred_element_type=F32)
        mine = early[j]
        finish(j, (sent + mine.astype(F32)).astype(BF16))
        return carry

    def finish_late(j, carry):
        hot, high = step_ids(j)
        picked = jnp.dot(choose(hot, high, LOCAL_PARTS + SENT_PARTS), table_rows(0, table.shape[0] * BLK), preferred_element_type=F32)
        finish(j, picked.astype(BF16))
        return carry

    lax.fori_loop(0, EARLY, finish_early, 0)
    lax.fori_loop(EARLY, blocks, finish_late, 0)

    ends[0] = block_at(normed_s, pos_s[0])
    ends[1] = block_at(normed_s, pos_s[blocks - 1])
    edges = [
        pltpu.make_async_remote_copy(
            src_ref=ends.at[source],
            dst_ref=far.at[slot],
            send_sem=send_sem.at[slot],
            recv_sem=recv_sem.at[slot],
            device_id=(space, peer),
            device_id_type=MESH,
        )
        for peer, source, slot in ((ctx + 1, 1, n_ctx), (ctx - 1, 0, n_ctx + 1))
    ]
    for side, edge in zip(sides[:2], edges):
        pl.when(side[0])(edge.start)
    if n_ctx - 1 > blocks:
        lax.fori_loop(blocks, n_ctx - 1, lambda j, carry: (start_send(j), carry)[1], 0)
    far[ctx] = block_at(normed_s, pos_s[pick_s[0, ctx, ctx]])
    for i, side in enumerate(sides[:2]):
        @pl.when(jnp.logical_not(side[1]))
        def _():
            far[n_ctx + i] = jnp.zeros((BLK, D), BF16)

    head_dim = D // HEADS
    heads = HALF // head_dim
    head_of = lane // head_dim
    scale = math.log2(math.e) / math.sqrt(head_dim)
    groups = D // HALF

    def spread(stacked):
        result = None
        for head in range(heads):
            part = stacked[head * BLK : (head + 1) * BLK]
            part = jnp.broadcast_to(part, (BLK, HALF))
            result = part if result is None else jnp.where(head_of == head, part, result)
        return result

    def attend(query, sources):
        def stack(ref, group):
            cols = slice(group * HALF, (group + 1) * HALF)
            return jnp.concatenate([ref[index, :, cols] for index in sources], 0)

        def score(group):
            part = query[:, group * HALF : (group + 1) * HALF]
            stacked = jnp.concatenate(
                [jnp.where(head_of == head, part, zero_like(part)) for head in range(heads)], 0
            )
            return lax.dot_general(
                stacked, stack(key_s, group), (((1,), (1,)), ((), ())), preferred_element_type=F32
            )

        ones = jnp.concatenate([block_at(ones_s, index) for index in sources], 0)
        results = []
        scores = [score(group) for group in range(groups)]
        for group in range(groups):
            peak = jnp.max(scores[group], axis=-1, keepdims=True)
            weights = jnp.exp2((scores[group] - peak) * scale).astype(BF16)
            mixed = jnp.dot(
                weights, jnp.concatenate([stack(value_s, group), ones], 1), preferred_element_type=F32
            )
            results.append((peak, mixed[:, :HALF], mixed[:, HALF:]))
        return results

    def near_blocks(b):
        return [pos_s[b - 1], pos_s[b], pos_s[b + 1]]

    def near(i, carry):
        b = i + 1
        at = pos_s[b]
        for group, (peak, total, den) in enumerate(attend(block_at(query_s, at), near_blocks(b))):
            cols = slice(group * HALF, (group + 1) * HALF)
            near_peak[i, :, cols] = spread(peak)
            near_sum[i, :, cols] = spread(total)
            near_den[i, :, cols] = spread(den)
        return carry

    lax.fori_loop(0, blocks - 2, near, 0)

    for j in range(n_ctx - 1):
        send(j).wait()
    for side, edge in zip(sides[:2], edges):
        pl.when(side[0])(edge.wait_send)
        pl.when(side[1])(edge.wait_recv)

    left, right = blocks + n_ctx, blocks + n_ctx + 1

    def project(s, valid, spare):
        both = jnp.dot(far[s], qkv_v[:, D:], preferred_element_type=F32)
        keys = both[:, :D]
        keep(blocks + s, keys, both[:, D:], valid, keys[:1] if spare is None else spare)

    def project_far(s, carry):
        project(s, lens_s[0, s * blocks + pick_s[0, s, ctx]], None)
        return carry

    lax.fori_loop(0, n_ctx, project_far, 0)
    for s, there, at, inner in (
        (n_ctx, ctx > 0, ctx * blocks - 1, 0),
        (n_ctx + 1, ctx < n_ctx - 1, (ctx + 1) * blocks, blocks - 1),
    ):
        valid = jnp.where(there, lens_s[0, jnp.where(there, at, 0)], 0)
        project(s, valid, block_at(key_s, pos_s[inner])[:1].astype(F32))

    def far_blocks(b):
        return [blocks + slots_s[0, k, b] for k in range(slots_s.shape[1])]

    def write(b, at, attended):
        out_ref[b] = (
            block_at(hidden_s, at)
            + jnp.dot(jnp.concatenate(attended, 1).astype(BF16), outw_v[...], preferred_element_type=F32)
        ).astype(BF16)

    def far_inner(i, carry):
        b = i + 1
        at = pos_s[b]
        attended = []
        for group, (peak, total, den) in enumerate(attend(block_at(query_s, at), far_blocks(b))):
            cols = slice(group * HALF, (group + 1) * HALF)
            peak, other = spread(peak), near_peak[i, :, cols]
            top = jnp.maximum(peak, other)
            mine, theirs = jnp.exp2((peak - top) * scale), jnp.exp2((other - top) * scale)
            attended.append(
                (spread(total) * mine + near_sum[i, :, cols] * theirs)
                / (spread(den) * mine + near_den[i, :, cols] * theirs)
            )
        write(b, at, attended)
        return carry

    lax.fori_loop(0, blocks - 2, far_inner, 0)

    def whole(i, carry):
        b = i * (blocks - 1)
        at = pos_s[b]
        before = jnp.where(i == 0, left, pos_s[jnp.maximum(b - 1, 0)])
        after = jnp.where(i == 0, pos_s[jnp.minimum(b + 1, blocks - 1)], right)
        results = attend(block_at(query_s, at), [before, at, after] + far_blocks(b))
        write(b, at, [spread(total) / spread(den) for _, total, den in results])
        return carry

    lax.fori_loop(0, 2, whole, 0)


def on_device(
    feats,
    face_rows,
    neighbours,
    block_len,
    dilated,
    pick,
    cpe_weight,
    cpe_bias,
    ln_gain,
    ln_bias,
    w_qkv,
    w_out,
):
    n_space, n_ctx = lax.axis_size("space"), lax.axis_size("ctx")
    count = feats.shape[1]
    blocks = count // BLK
    kept = blocks + n_ctx + 2
    operands = (
        feats.reshape(blocks, BLK, D), face_rows, neighbours.transpose(2, 0, 1).reshape(OFFSETS, blocks, 1, BLK), block_len, dilated.transpose(0, 2, 1), pick,
        cpe_weight.reshape(-1, D), cpe_bias[None], ln_gain[None], ln_bias[None], w_qkv, w_out,
    )
    operands = [pltpu.with_memory_space_constraint(operand, pltpu.HBM) for operand in operands]
    shape = lambda i: operands[i].shape
    return pl.pallas_call(
        functools.partial(body, n_space, n_ctx),
        in_specs=[pl.BlockSpec(memory_space=pltpu.HBM)] * len(operands),
        out_specs=pl.BlockSpec(memory_space=pltpu.VMEM),
        out_shape=jax.ShapeDtypeStruct((blocks, BLK, D), BF16),
        scratch_shapes=[
            pltpu.VMEM(((count + 2 * EDGE + 3 * FACE) // BLK, BLK, D), BF16),
            pltpu.VMEM(shape(1), jnp.int32),
            pltpu.VMEM(shape(2), jnp.int32),
            pltpu.VMEM(shape(6), BF16),
            pltpu.VMEM(shape(7), F32),
            pltpu.VMEM(shape(8), F32),
            pltpu.VMEM(shape(9), F32),
            pltpu.VMEM(shape(10), BF16),
            pltpu.VMEM(shape(11), BF16),
            pltpu.SMEM(shape(3), jnp.int32),
            pltpu.SMEM(shape(4), jnp.int32),
            pltpu.SMEM(shape(5), jnp.int32),
            pltpu.SMEM((blocks,), jnp.int32),
            pltpu.SMEM((blocks,), jnp.int32),
            pltpu.VMEM((EARLY, OFFSETS * BLK, D), BF16),
            pltpu.VMEM((blocks, BLK, D), F32),
            pltpu.VMEM((blocks, BLK, D), BF16),
            pltpu.VMEM((blocks, BLK, D), BF16),
            pltpu.VMEM((kept, BLK, D), BF16),
            pltpu.VMEM((kept, BLK, D), BF16),
            pltpu.VMEM((kept, BLK, HALF), BF16),
            pltpu.VMEM((n_ctx, BLK, D), BF16),
            pltpu.VMEM((2, BLK, D), BF16),
            pltpu.VMEM((n_ctx + 2, BLK, D), BF16),
            pltpu.VMEM((blocks - 2, BLK, D), F32),
            pltpu.VMEM((blocks - 2, BLK, D), F32),
            pltpu.VMEM((blocks - 2, BLK, D), F32),
            pltpu.SemaphoreType.DMA((len(operands),)),
            pltpu.SemaphoreType.DMA((4,)),
            pltpu.SemaphoreType.DMA((4,)),
            pltpu.SemaphoreType.DMA((n_ctx + 2,)),
            pltpu.SemaphoreType.DMA((n_ctx + 2,)),
        ],
        compiler_params=pltpu.CompilerParams(
            collective_id=0, has_side_effects=True, vmem_limit_bytes=48 * 2**20
        ),
    )(*operands).reshape(1, count, D)


def solution(mesh):
    placed = (
        P("space", "ctx", None),
        P("space", "ctx"),
        P("space", "ctx", None),
        P("space", None),
        P("space", "ctx", None),
        P("space", None, None),
        P(),
        P(),
        P(),
        P(),
        P(),
        P(),
    )
    return jax.shard_map(
        on_device, mesh=mesh, in_specs=placed, out_specs=P("space", "ctx", None), check_vma=False
    )
```

```python
import functools
import math

import jax
import jax.numpy as jnp
from jax import lax
from jax.experimental import pallas as pl
from jax.experimental.pallas import tpu as pltpu
from jax.sharding import PartitionSpec as P

D = 256
HEADS = 8
BLK = 128
EDGE = 128
FACE = 256
HALF = 128
OFFSETS = 6

MESH = pl.DeviceIdType.MESH
BF16 = jnp.bfloat16
F32 = jnp.float32

LOCAL_PARTS = tuple(range(1, 9)) + (12, 13)
SENT_PARTS = (0, 9, 10, 11, 14, 15)
EARLY = 4
FIRST = 4


def zero_like(value):
    return jnp.zeros_like(value)


def body(
    n_space, n_ctx,
    feats, face_rows, neighbours, block_len, dilated, pick, cpe_weight, cpe_bias, ln_gain, ln_bias, w_qkv, w_out,
    out_ref,
    table, rows_v, ids_v, weight_v, bias_v, gain_v, shift_v, qkv_v, outw_v,
    lens_s, slots_s, pick_s, pos_s, perm_s,
    hidden_s, query_s, normed_s, key_s, value_s, ones_s, outgoing, ends, far,
    near_peak, near_sum, near_den, picked_s, scores_a, scores_b,
    load_sem, table_send, table_recv, send_sem, recv_sem,
):
    space, ctx = lax.axis_index("space"), lax.axis_index("ctx")
    blocks = feats.shape[0]
    count = blocks * BLK
    local = count + FACE

    scores_s = (scores_a, scores_b)
    barrier = pltpu.get_barrier_semaphore()

    def ctx_peer(j):
        half = n_ctx // 2
        mine = ctx // half
        other = (1 - mine) * half + lax.rem(ctx + j, half)
        same = mine * half + lax.rem(ctx + j + 1, half)
        return jnp.where(j < half, other, same)

    for j in range(n_ctx - 1):
        pl.semaphore_signal(barrier, inc=1, device_id=(space, ctx_peer(j)), device_id_type=MESH)
    sides = (
        (ctx < n_ctx - 1, ctx > 0, (space, ctx + 1)),
        (ctx > 0, ctx < n_ctx - 1, (space, ctx - 1)),
        (space < n_space - 1, space > 0, (space + 1, ctx)),
        (space > 0, space < n_space - 1, (space - 1, ctx)),
    )
    for there, _, peer in sides[2:]:
        @pl.when(there)
        def _():
            pl.semaphore_signal(barrier, inc=1, device_id=peer, device_id_type=MESH)

    loads = [
        pltpu.make_async_copy(source, target, load_sem.at[i])
        for i, (source, target) in enumerate((
            (feats, table.at[pl.ds(0, blocks)]),
            (face_rows, rows_v),
            (pick, pick_s),
            (neighbours, ids_v),
            (block_len, lens_s),
            (dilated, slots_s),
            (cpe_weight, weight_v),
            (cpe_bias, bias_v),
            (ln_gain, gain_v),
            (ln_bias, shift_v),
            (w_qkv, qkv_v),
            (w_out, outw_v),
        ))
    ]
    for load in loads[:FIRST]:
        load.start()

    lane = lax.broadcasted_iota(jnp.int32, (BLK, HALF), 1)
    row = lax.broadcasted_iota(jnp.int32, (BLK, 1), 0)

    def split_ids(columns):
        spread = jnp.concatenate([jnp.broadcast_to(ids, (BLK, BLK)).T for ids in columns], 0)
        lanes = lax.broadcasted_iota(jnp.int32, spread.shape, 1)
        hot = jnp.where((spread & (BLK - 1)) == lanes, 1.0, 0.0).astype(BF16)
        return hot, (spread >> 7).astype(F32).astype(BF16)

    def choose(hot, high, parts):
        return jnp.concatenate([jnp.where(high == BF16(part), hot, zero_like(hot)) for part in parts], 1)

    loads[0].wait()
    loads[1].wait()
    hot, high = split_ids([rows_v[:, i * BLK : (i + 1) * BLK] for i in range(FACE // BLK)])
    table[blocks : local // BLK] = jnp.dot(
        choose(hot, high, range(blocks)), table[:blocks].reshape(count, D), preferred_element_type=F32
    ).astype(BF16).reshape(FACE // BLK, BLK, D)

    for load in loads[FIRST:]:
        load.start()
    pl.semaphore_wait(
        barrier, n_ctx - 1 + sides[2][0].astype(jnp.int32) + sides[3][0].astype(jnp.int32)
    )
    pieces = (
        (count - EDGE, local, EDGE),
        (0, local + EDGE, EDGE),
        (count, local + 2 * EDGE, FACE),
        (count, local + 2 * EDGE + FACE, FACE),
    )
    copies = [
        pltpu.make_async_remote_copy(
            src_ref=table.at[pl.ds(source // BLK, size // BLK)],
            dst_ref=table.at[pl.ds(target // BLK, size // BLK)],
            send_sem=table_send.at[i],
            recv_sem=table_recv.at[i],
            device_id=sides[i][2],
            device_id_type=MESH,
        )
        for i, (source, target, size) in enumerate(pieces)
    ]
    for i in (2, 3, 0, 1):
        pl.when(sides[i][0])(copies[i].start)
    for i, (_, target, size) in enumerate(pieces):
        @pl.when(jnp.logical_not(sides[i][1]))
        def _():
            table[target // BLK : (target + size) // BLK] = jnp.zeros((size // BLK, BLK, D), BF16)

    loads[2].wait()
    wanted = [pick_s[0, ctx, ctx_peer(j)] for j in range(n_ctx)]
    need = [jnp.int32(n_ctx + b) for b in range(blocks)]
    for j in reversed(range(n_ctx)):
        need = [jnp.where(wanted[j] == b, j, need[b]) for b in range(blocks)]
    position = [
        sum((need[a] < need[b]).astype(jnp.int32) for a in range(blocks) if a != b) for b in range(blocks)
    ]
    for b in range(blocks):
        pos_s[b] = position[b]
    for j in range(blocks):
        perm_s[j] = sum(jnp.where(position[b] == j, b, 0) for b in range(blocks))

    for load in loads[3:]:
        load.wait()

    def block_at(ref, index):
        return ref[index]

    def table_rows(first, last):
        return table[first // BLK : last // BLK].reshape(last - first, D)

    def step_ids(j):
        at = perm_s[j]
        return split_ids([ids_v[o, at] for o in range(OFFSETS)])

    def pick_early(j, carry):
        hot, high = step_ids(j)
        picked_s[j] = jnp.dot(
            choose(hot, high, LOCAL_PARTS), table_rows(0, local), preferred_element_type=F32
        ).astype(BF16)
        return carry

    lax.fori_loop(0, EARLY, pick_early, 0)

    for i in range(4):
        pl.when(sides[i][0])(copies[i].wait_send)
        pl.when(sides[i][1])(copies[i].wait_recv)

    def keep(index, keys, values, valid, spare):
        inside = row < valid
        key_s[index] = jnp.where(inside, keys, spare).astype(BF16)
        value_s[index] = jnp.where(inside, values, 0.0).astype(BF16)
        ones_s[index] = jnp.where(jnp.broadcast_to(inside, (BLK, HALF)), 1.0, 0.0).astype(BF16)

    def send(j):
        return pltpu.make_async_remote_copy(
            src_ref=outgoing.at[j],
            dst_ref=far.at[ctx],
            send_sem=send_sem.at[j],
            recv_sem=recv_sem.at[j],
            device_id=(space, ctx_peer(j)),
            device_id_type=MESH,
        )

    def start_send(j):
        outgoing[j] = block_at(normed_s, pos_s[pick_s[0, ctx, ctx_peer(j)]])
        send(j).start()

    def finish(first, last):
        steps = range(first, last)
        order = [perm_s[j] for j in steps]
        own = jnp.concatenate([table[block] for block in order], 0)
        taps = jnp.concatenate(
            [own]
            + [jnp.concatenate([picked_s[j, o * BLK : (o + 1) * BLK] for j in steps], 0) for o in range(OFFSETS)],
            1,
        )
        conv = jnp.dot(taps, weight_v[...], preferred_element_type=F32)
        hidden = own.astype(F32) + conv + bias_v[...]
        center = hidden - jnp.mean(hidden, axis=-1, keepdims=True)
        variance = jnp.mean(center * center, axis=-1, keepdims=True)
        normed = (center * lax.rsqrt(variance + 1e-05) * gain_v[...] + shift_v[...]).astype(BF16)
        for b, j in enumerate(steps):
            normed_s[j] = normed[b * BLK : (b + 1) * BLK]
        for j in steps:
            if j < n_ctx - 1:
                start_send(j)
        projected = jnp.dot(normed, qkv_v[...], preferred_element_type=F32)
        for b, j in enumerate(steps):
            part = slice(b * BLK, (b + 1) * BLK)
            hidden_s[j] = hidden[part]
            query_s[j] = projected[part, :D].astype(BF16)
            keys = projected[part, D : 2 * D]
            keep(j, keys, projected[part, 2 * D :], lens_s[0, ctx * blocks + order[b]], keys[:1])

    def pick_sent(j, carry):
        hot, high = step_ids(j)
        sent = jnp.dot(
            choose(hot, high, SENT_PARTS), table_rows(local, table.shape[0] * BLK), preferred_element_type=F32
        )
        picked_s[j] = (sent + picked_s[j].astype(F32)).astype(BF16)
        return carry

    def pick_late(j, carry):
        hot, high = step_ids(j)
        picked_s[j] = jnp.dot(
            choose(hot, high, LOCAL_PARTS + SENT_PARTS), table_rows(0, table.shape[0] * BLK),
            preferred_element_type=F32,
        ).astype(BF16)
        return carry

    lax.fori_loop(0, 1, pick_sent, 0)
    finish(0, 1)
    lax.fori_loop(1, EARLY, pick_sent, 0)
    finish(1, EARLY)
    lax.fori_loop(EARLY, blocks, pick_late, 0)
    finish(EARLY, blocks)

    ends[0] = block_at(normed_s, pos_s[0])
    ends[1] = block_at(normed_s, pos_s[blocks - 1])
    edges = [
        pltpu.make_async_remote_copy(
            src_ref=ends.at[source],
            dst_ref=far.at[slot],
            send_sem=send_sem.at[slot],
            recv_sem=recv_sem.at[slot],
            device_id=(space, peer),
            device_id_type=MESH,
        )
        for peer, source, slot in ((ctx + 1, 1, n_ctx), (ctx - 1, 0, n_ctx + 1))
    ]
    for side, edge in zip(sides[:2], edges):
        pl.when(side[0])(edge.start)
    if n_ctx - 1 > blocks:
        lax.fori_loop(blocks, n_ctx - 1, lambda j, carry: (start_send(j), carry)[1], 0)
    far[ctx] = block_at(normed_s, pos_s[pick_s[0, ctx, ctx]])
    for i, side in enumerate(sides[:2]):
        @pl.when(jnp.logical_not(side[1]))
        def _():
            far[n_ctx + i] = jnp.zeros((BLK, D), BF16)

    head_dim = D // HEADS
    heads = HALF // head_dim
    head_of = lane // head_dim
    scale = math.log2(math.e) / math.sqrt(head_dim)
    groups = D // HALF

    def spread(stacked):
        result = None
        for head in range(heads):
            part = stacked[head * BLK : (head + 1) * BLK]
            part = jnp.broadcast_to(part, (BLK, HALF))
            result = part if result is None else jnp.where(head_of == head, part, result)
        return result

    def stack(ref, sources, group):
        cols = slice(group * HALF, (group + 1) * HALF)
        return jnp.concatenate([ref[index, :, cols] for index in sources], 0)

    def score(at, sources, group):
        part = query_s[at, :, group * HALF : (group + 1) * HALF]
        stacked = jnp.concatenate(
            [jnp.where(head_of == head, part, zero_like(part)) for head in range(heads)], 0
        )
        scores_s[group][:, : len(sources) * BLK] = lax.dot_general(
            stacked, stack(key_s, sources, group), (((1,), (1,)), ((), ())), preferred_element_type=F32
        )

    def weigh(sources, group):
        scores = scores_s[group][:, : len(sources) * BLK]
        peak = jnp.max(scores, axis=-1, keepdims=True)
        weights = jnp.exp2((scores - peak) * scale).astype(BF16)
        ones = jnp.concatenate([ones_s[index] for index in sources], 0)
        mixed = jnp.dot(
            weights, jnp.concatenate([stack(value_s, sources, group), ones], 1), preferred_element_type=F32
        )
        return peak, mixed[:, :HALF], mixed[:, HALF:]

    def attend(at, sources, then):
        score(at, sources, 1)
        first = weigh(sources, 0)
        if then is not None:
            score(*then, 0)
        return [first, weigh(sources, 1)]

    def near_blocks(b):
        return [pos_s[b - 1], pos_s[b], pos_s[b + 1]]

    def near(i, carry):
        b = i + 1
        after = jnp.minimum(b + 1, blocks - 2)
        at = pos_s[b]
        for group, (peak, total, den) in enumerate(attend(at, near_blocks(b), (pos_s[after], near_blocks(after)))):
            cols = slice(group * HALF, (group + 1) * HALF)
            near_peak[i, :, cols] = spread(peak)
            near_sum[i, :, cols] = spread(total)
            near_den[i, :, cols] = spread(den)
        return carry

    score(pos_s[1], near_blocks(1), 0)
    lax.fori_loop(0, blocks - 2, near, 0)

    for j in range(n_ctx - 1):
        send(j).wait()

    left, right = blocks + n_ctx, blocks + n_ctx + 1

    def project(first, last):
        return jnp.dot(
            far[first:last].reshape((last - first) * BLK, D), qkv_v[:, D:], preferred_element_type=F32
        )

    def keep_far(s, both, valid, spare):
        keys = both[:, :D]
        keep(blocks + s, keys, both[:, D:], valid, keys[:1] if spare is None else spare)

    arrived = project(0, n_ctx)

    for s in range(n_ctx):
        keep_far(s, arrived[s * BLK : (s + 1) * BLK], lens_s[0, s * blocks + pick_s[0, s, ctx]], None)
    def far_blocks(b):
        return [blocks + slots_s[0, k, b] for k in range(slots_s.shape[1])]

    def write(b, at, attended):
        out_ref[b] = (
            block_at(hidden_s, at)
            + jnp.dot(jnp.concatenate(attended, 1).astype(BF16), outw_v[...], preferred_element_type=F32)
        ).astype(BF16)

    def far_inner(i, carry):
        b = i + 1
        after = jnp.minimum(b + 1, blocks - 2)
        at = pos_s[b]
        attended = []
        for group, (peak, total, den) in enumerate(attend(at, far_blocks(b), (pos_s[after], far_blocks(after)))):
            cols = slice(group * HALF, (group + 1) * HALF)
            peak, other = spread(peak), near_peak[i, :, cols]
            top = jnp.maximum(peak, other)
            mine, theirs = jnp.exp2((peak - top) * scale), jnp.exp2((other - top) * scale)
            attended.append(
                (spread(total) * mine + near_sum[i, :, cols] * theirs)
                / (spread(den) * mine + near_den[i, :, cols] * theirs)
            )
        write(b, at, attended)
        return carry

    score(pos_s[1], far_blocks(1), 0)
    lax.fori_loop(0, blocks - 2, far_inner, 0)

    for side, edge in zip(sides[:2], edges):
        pl.when(side[0])(edge.wait_send)
        pl.when(side[1])(edge.wait_recv)
    arrived = project(n_ctx, n_ctx + 2)
    for s, there, at, inner in (
        (n_ctx, ctx > 0, ctx * blocks - 1, 0),
        (n_ctx + 1, ctx < n_ctx - 1, (ctx + 1) * blocks, blocks - 1),
    ):
        valid = jnp.where(there, lens_s[0, jnp.where(there, at, 0)], 0)
        keep_far(s, arrived[(s - n_ctx) * BLK : (s - n_ctx + 1) * BLK], valid, block_at(key_s, pos_s[inner])[:1].astype(F32))

    def whole(i, carry):
        b = i * (blocks - 1)
        before = jnp.where(i == 0, left, pos_s[jnp.maximum(b - 1, 0)])
        after = jnp.where(i == 0, pos_s[jnp.minimum(b + 1, blocks - 1)], right)
        sources = [before, pos_s[b], after] + far_blocks(b)
        score(pos_s[b], sources, 0)
        results = attend(pos_s[b], sources, None)
        write(b, pos_s[b], [spread(total) / spread(den) for _, total, den in results])
        return carry

    lax.fori_loop(0, 2, whole, 0)


def on_device(
    feats,
    face_rows,
    neighbours,
    block_len,
    dilated,
    pick,
    cpe_weight,
    cpe_bias,
    ln_gain,
    ln_bias,
    w_qkv,
    w_out,
):
    n_space, n_ctx = lax.axis_size("space"), lax.axis_size("ctx")
    count = feats.shape[1]
    blocks = count // BLK
    kept = blocks + n_ctx + 2
    operands = (
        feats.reshape(blocks, BLK, D), face_rows, neighbours.transpose(2, 0, 1).reshape(OFFSETS, blocks, 1, BLK), block_len, dilated.transpose(0, 2, 1), pick,
        cpe_weight.reshape(-1, D), cpe_bias[None], ln_gain[None], ln_bias[None], w_qkv, w_out,
    )
    operands = [pltpu.with_memory_space_constraint(operand, pltpu.HBM) for operand in operands]
    shape = lambda i: operands[i].shape
    return pl.pallas_call(
        functools.partial(body, n_space, n_ctx),
        in_specs=[pl.BlockSpec(memory_space=pltpu.HBM)] * len(operands),
        out_specs=pl.BlockSpec(memory_space=pltpu.VMEM),
        out_shape=jax.ShapeDtypeStruct((blocks, BLK, D), BF16),
        scratch_shapes=[
            pltpu.VMEM(((count + 2 * EDGE + 3 * FACE) // BLK, BLK, D), BF16),
            pltpu.VMEM(shape(1), jnp.int32),
            pltpu.VMEM(shape(2), jnp.int32),
            pltpu.VMEM(shape(6), BF16),
            pltpu.VMEM(shape(7), F32),
            pltpu.VMEM(shape(8), F32),
            pltpu.VMEM(shape(9), F32),
            pltpu.VMEM(shape(10), BF16),
            pltpu.VMEM(shape(11), BF16),
            pltpu.SMEM(shape(3), jnp.int32),
            pltpu.SMEM(shape(4), jnp.int32),
            pltpu.SMEM(shape(5), jnp.int32),
            pltpu.SMEM((blocks,), jnp.int32),
            pltpu.SMEM((blocks,), jnp.int32),
            pltpu.VMEM((blocks, BLK, D), F32),
            pltpu.VMEM((blocks, BLK, D), BF16),
            pltpu.VMEM((blocks, BLK, D), BF16),
            pltpu.VMEM((kept, BLK, D), BF16),
            pltpu.VMEM((kept, BLK, D), BF16),
            pltpu.VMEM((kept, BLK, HALF), BF16),
            pltpu.VMEM((n_ctx, BLK, D), BF16),
            pltpu.VMEM((2, BLK, D), BF16),
            pltpu.VMEM((n_ctx + 2, BLK, D), BF16),
            pltpu.VMEM((blocks - 2, BLK, D), F32),
            pltpu.VMEM((blocks - 2, BLK, D), F32),
            pltpu.VMEM((blocks - 2, BLK, D), F32),
            pltpu.VMEM((blocks, OFFSETS * BLK, D), BF16),
            pltpu.VMEM((HALF * HEADS // D * BLK, 7 * BLK), F32),
            pltpu.VMEM((HALF * HEADS // D * BLK, 7 * BLK), F32),
            pltpu.SemaphoreType.DMA((len(operands),)),
            pltpu.SemaphoreType.DMA((4,)),
            pltpu.SemaphoreType.DMA((4,)),
            pltpu.SemaphoreType.DMA((n_ctx + 2,)),
            pltpu.SemaphoreType.DMA((n_ctx + 2,)),
        ],
        compiler_params=pltpu.CompilerParams(
            collective_id=0, has_side_effects=True, vmem_limit_bytes=48 * 2**20
        ),
    )(*operands).reshape(1, count, D)


def solution(mesh):
    placed = (
        P("space", "ctx", None),
        P("space", "ctx"),
        P("space", "ctx", None),
        P("space", None),
        P("space", "ctx", None),
        P("space", None, None),
        P(),
        P(),
        P(),
        P(),
        P(),
        P(),
    )
    return jax.shard_map(
        on_device, mesh=mesh, in_specs=placed, out_specs=P("space", "ctx", None), check_vma=False
    )
```

```python
import functools
import math

import jax
import jax.numpy as jnp
from jax import lax
from jax.experimental import pallas as pl
from jax.experimental.pallas import tpu as pltpu
from jax.sharding import PartitionSpec as P

D = 256
HEADS = 8
BLK = 128
EDGE = 128
FACE = 256
HALF = 128
OFFSETS = 6

MESH = pl.DeviceIdType.MESH
BF16 = jnp.bfloat16
F32 = jnp.float32

LOCAL_PARTS = tuple(range(1, 9)) + (12, 13)
SENT_PARTS = (0, 9, 10, 11, 14, 15)
EARLY = 6
GROUPS = (1, 4, 8)


def zero_like(value):
    return jnp.zeros_like(value)


def body(
    n_space, n_ctx,
    feats, face_rows, neighbours, block_len, dilated, pick, cpe_weight, cpe_bias, ln_gain, ln_bias, w_qkv, w_out,
    out_ref,
    table, rows_v, ids_v, weight_v, bias_v, gain_v, shift_v, qkv_v, outw_v,
    lens_s, slots_s, pick_s, pos_s, perm_s,
    hidden_s, query_s, normed_s, key_s, value_s, ones_s, outgoing, ends, far,
    near_peak, near_sum, near_den, picked_s, hot_s, high_s, scores_a, scores_b,
    load_sem, table_send, table_recv, send_sem, recv_sem,
):
    space, ctx = lax.axis_index("space"), lax.axis_index("ctx")
    blocks = feats.shape[0]
    count = blocks * BLK
    local = count + FACE

    scores_s = (scores_a, scores_b)
    barrier = pltpu.get_barrier_semaphore()

    def ctx_peer(j):
        turn = (j + 1) // 2
        return lax.rem(ctx + n_ctx // 2 + (n_ctx - turn if j % 2 else turn), n_ctx)

    for j in range(n_ctx - 1):
        pl.semaphore_signal(barrier, inc=1, device_id=(space, ctx_peer(j)), device_id_type=MESH)
    sides = (
        (ctx < n_ctx - 1, ctx > 0, (space, ctx + 1)),
        (ctx > 0, ctx < n_ctx - 1, (space, ctx - 1)),
        (space < n_space - 1, space > 0, (space + 1, ctx)),
        (space > 0, space < n_space - 1, (space - 1, ctx)),
    )
    for there, _, peer in sides[2:]:
        @pl.when(there)
        def _():
            pl.semaphore_signal(barrier, inc=1, device_id=peer, device_id_type=MESH)

    loads = [
        pltpu.make_async_copy(source, target, load_sem.at[i])
        for i, (source, target) in enumerate((
            (feats, table.at[pl.ds(0, blocks)]),
            (face_rows, rows_v),
            (pick, pick_s),
            (neighbours, ids_v),
            (block_len, lens_s),
            (dilated, slots_s),
            (cpe_weight, weight_v),
            (cpe_bias, bias_v),
            (ln_gain, gain_v),
            (ln_bias, shift_v),
            (w_qkv, qkv_v),
            (w_out, outw_v),
        ))
    ]
    for load in loads:
        load.start()

    lane = lax.broadcasted_iota(jnp.int32, (BLK, HALF), 1)
    row = lax.broadcasted_iota(jnp.int32, (BLK, 1), 0)

    def split_ids(columns):
        spread = jnp.concatenate([jnp.broadcast_to(ids, (BLK, BLK)).T for ids in columns], 0)
        lanes = lax.broadcasted_iota(jnp.int32, spread.shape, 1)
        hot = jnp.where((spread & (BLK - 1)) == lanes, 1.0, 0.0).astype(BF16)
        return hot, (spread >> 7).astype(F32).astype(BF16)

    def choose(hot, high, parts):
        return jnp.concatenate([jnp.where(high == BF16(part), hot, zero_like(hot)) for part in parts], 1)

    loads[0].wait()
    loads[1].wait()
    hot, high = split_ids([rows_v[:, i * BLK : (i + 1) * BLK] for i in range(FACE // BLK)])
    table[blocks : local // BLK] = jnp.dot(
        choose(hot, high, range(blocks)), table[:blocks].reshape(count, D), preferred_element_type=F32
    ).astype(BF16).reshape(FACE // BLK, BLK, D)

    pl.semaphore_wait(
        barrier, n_ctx - 1 + sides[2][0].astype(jnp.int32) + sides[3][0].astype(jnp.int32)
    )
    pieces = (
        (count - EDGE, local, EDGE),
        (0, local + EDGE, EDGE),
        (count, local + 2 * EDGE, FACE),
        (count, local + 2 * EDGE + FACE, FACE),
    )
    copies = [
        pltpu.make_async_remote_copy(
            src_ref=table.at[pl.ds(source // BLK, size // BLK)],
            dst_ref=table.at[pl.ds(target // BLK, size // BLK)],
            send_sem=table_send.at[i],
            recv_sem=table_recv.at[i],
            device_id=sides[i][2],
            device_id_type=MESH,
        )
        for i, (source, target, size) in enumerate(pieces)
    ]
    for i in (2, 3, 0, 1):
        pl.when(sides[i][0])(copies[i].start)
    for i, (_, target, size) in enumerate(pieces):
        @pl.when(jnp.logical_not(sides[i][1]))
        def _():
            table[target // BLK : (target + size) // BLK] = jnp.zeros((size // BLK, BLK, D), BF16)

    loads[2].wait()
    wanted = [pick_s[0, ctx, ctx_peer(j)] for j in range(n_ctx)]
    need = [jnp.int32(n_ctx + b) for b in range(blocks)]
    for j in reversed(range(n_ctx)):
        need = [jnp.where(wanted[j] == b, j, need[b]) for b in range(blocks)]
    position = [
        sum((need[a] < need[b]).astype(jnp.int32) for a in range(blocks) if a != b) for b in range(blocks)
    ]
    for b in range(blocks):
        pos_s[b] = position[b]
    for j in range(blocks):
        perm_s[j] = sum(jnp.where(position[b] == j, b, 0) for b in range(blocks))

    for load in loads[3:]:
        load.wait()

    def block_at(ref, index):
        return ref[index]

    def table_rows(first, last):
        return table[first // BLK : last // BLK].reshape(last - first, D)

    def step_ids(j):
        at = perm_s[j]
        return split_ids([ids_v[o, at] for o in range(OFFSETS)])

    def pick_early(j, carry):
        hot, high = hot_s[j], high_s[j] = step_ids(j)
        picked_s[j] = jnp.dot(
            choose(hot, high, LOCAL_PARTS), table_rows(0, local), preferred_element_type=F32
        ).astype(BF16)
        return carry

    lax.fori_loop(0, EARLY, pick_early, 0, unroll=2)

    for i in range(4):
        pl.when(sides[i][0])(copies[i].wait_send)
        pl.when(sides[i][1])(copies[i].wait_recv)

    def keep(index, keys, values, valid, spare):
        inside = row < valid
        key_s[index] = jnp.where(inside, keys, spare).astype(BF16)
        value_s[index] = jnp.where(inside, values, 0.0).astype(BF16)
        ones_s[index] = jnp.where(jnp.broadcast_to(inside, (BLK, HALF)), 1.0, 0.0).astype(BF16)

    def send(j):
        return pltpu.make_async_remote_copy(
            src_ref=outgoing.at[j],
            dst_ref=far.at[ctx],
            send_sem=send_sem.at[j],
            recv_sem=recv_sem.at[j],
            device_id=(space, ctx_peer(j)),
            device_id_type=MESH,
        )

    def start_send(j):
        outgoing[j] = block_at(normed_s, pos_s[pick_s[0, ctx, ctx_peer(j)]])
        send(j).start()

    def finish(first, last):
        steps = range(first, last)
        order = [perm_s[j] for j in steps]
        own = jnp.concatenate([table[block] for block in order], 0)
        taps = jnp.concatenate(
            [own]
            + [jnp.concatenate([picked_s[j, o * BLK : (o + 1) * BLK] for j in steps], 0) for o in range(OFFSETS)],
            1,
        )
        conv = jnp.dot(taps, weight_v[...], preferred_element_type=F32)
        hidden = own.astype(F32) + conv + bias_v[...]
        center = hidden - jnp.mean(hidden, axis=-1, keepdims=True)
        variance = jnp.mean(center * center, axis=-1, keepdims=True)
        normed = (center * lax.rsqrt(variance + 1e-05) * gain_v[...] + shift_v[...]).astype(BF16)
        for b, j in enumerate(steps):
            normed_s[j] = normed[b * BLK : (b + 1) * BLK]
        for j in steps:
            if j < n_ctx - 1:
                start_send(j)
        projected = jnp.dot(normed, qkv_v[...], preferred_element_type=F32)
        for b, j in enumerate(steps):
            part = slice(b * BLK, (b + 1) * BLK)
            hidden_s[j] = hidden[part]
            query_s[j] = projected[part, :D].astype(BF16)
            keys = projected[part, D : 2 * D]
            keep(j, keys, projected[part, 2 * D :], lens_s[0, ctx * blocks + order[b]], keys[:1])

    def pick_sent(j, carry):
        hot, high = hot_s[j], high_s[j]
        sent = jnp.dot(
            choose(hot, high, SENT_PARTS), table_rows(local, table.shape[0] * BLK), preferred_element_type=F32
        )
        picked_s[j] = (sent + picked_s[j].astype(F32)).astype(BF16)
        return carry

    def pick_late(j, carry):
        hot, high = step_ids(j)
        picked_s[j] = jnp.dot(
            choose(hot, high, LOCAL_PARTS + SENT_PARTS), table_rows(0, table.shape[0] * BLK),
            preferred_element_type=F32,
        ).astype(BF16)
        return carry

    first = 0
    for last in GROUPS:
        if first < EARLY:
            lax.fori_loop(first, min(last, EARLY), pick_sent, 0, unroll=True)
        if last > EARLY:
            lax.fori_loop(max(first, EARLY), last, pick_late, 0, unroll=2)
        finish(first, last)
        first = last

    ends[0] = block_at(normed_s, pos_s[0])
    ends[1] = block_at(normed_s, pos_s[blocks - 1])
    edges = [
        pltpu.make_async_remote_copy(
            src_ref=ends.at[source],
            dst_ref=far.at[slot],
            send_sem=send_sem.at[slot],
            recv_sem=recv_sem.at[slot],
            device_id=(space, peer),
            device_id_type=MESH,
        )
        for peer, source, slot in ((ctx + 1, 1, n_ctx), (ctx - 1, 0, n_ctx + 1))
    ]
    for side, edge in zip(sides[:2], edges):
        pl.when(side[0])(edge.start)
    for j in range(blocks, n_ctx - 1):
        start_send(j)
    far[ctx] = block_at(normed_s, pos_s[pick_s[0, ctx, ctx]])
    for i, side in enumerate(sides[:2]):
        @pl.when(jnp.logical_not(side[1]))
        def _():
            far[n_ctx + i] = jnp.zeros((BLK, D), BF16)

    head_dim = D // HEADS
    heads = HALF // head_dim
    head_of = lane // head_dim
    scale = math.log2(math.e) / math.sqrt(head_dim)
    groups = D // HALF

    def spread(stacked):
        result = None
        for head in range(heads):
            part = stacked[head * BLK : (head + 1) * BLK]
            part = jnp.broadcast_to(part, (BLK, HALF))
            result = part if result is None else jnp.where(head_of == head, part, result)
        return result

    def stack(ref, sources, group):
        cols = slice(group * HALF, (group + 1) * HALF)
        return jnp.concatenate([ref[index, :, cols] for index in sources], 0)

    def score(at, sources, group):
        part = query_s[at, :, group * HALF : (group + 1) * HALF]
        stacked = jnp.concatenate(
            [jnp.where(head_of == head, part, zero_like(part)) for head in range(heads)], 0
        )
        scores_s[group][:, : len(sources) * BLK] = lax.dot_general(
            stacked, stack(key_s, sources, group), (((1,), (1,)), ((), ())), preferred_element_type=F32
        )

    def weigh(sources, group):
        scores = scores_s[group][:, : len(sources) * BLK]
        peak = jnp.max(scores, axis=-1, keepdims=True)
        weights = jnp.exp2((scores - peak) * scale).astype(BF16)
        ones = jnp.concatenate([ones_s[index] for index in sources], 0)
        mixed = jnp.dot(
            weights, jnp.concatenate([stack(value_s, sources, group), ones], 1), preferred_element_type=F32
        )
        return peak, mixed[:, :HALF], mixed[:, HALF:]

    def attend(at, sources, then):
        score(at, sources, 1)
        first = weigh(sources, 0)
        if then is not None:
            score(*then, 0)
        return [first, weigh(sources, 1)]

    def near_blocks(b):
        return [pos_s[b - 1], pos_s[b], pos_s[b + 1]]

    def near(i, carry):
        b = i + 1
        after = jnp.minimum(b + 1, blocks - 2)
        at = pos_s[b]
        for group, (peak, total, den) in enumerate(attend(at, near_blocks(b), (pos_s[after], near_blocks(after)))):
            cols = slice(group * HALF, (group + 1) * HALF)
            near_peak[i, :, cols] = spread(peak)
            near_sum[i, :, cols] = spread(total)
            near_den[i, :, cols] = spread(den)
        return carry

    score(pos_s[1], near_blocks(1), 0)
    lax.fori_loop(0, blocks - 2, near, 0, unroll=2)

    for j in range(n_ctx - 1):
        send(j).wait()

    left, right = blocks + n_ctx, blocks + n_ctx + 1

    def project(first, last):
        return jnp.dot(
            far[first:last].reshape((last - first) * BLK, D), qkv_v[:, D:], preferred_element_type=F32
        )

    def keep_far(s, both, valid, spare):
        keys = both[:, :D]
        keep(blocks + s, keys, both[:, D:], valid, keys[:1] if spare is None else spare)

    arrived = project(0, n_ctx)

    for s in range(n_ctx):
        keep_far(s, arrived[s * BLK : (s + 1) * BLK], lens_s[0, s * blocks + pick_s[0, s, ctx]], None)
    def far_blocks(b):
        return [blocks + slots_s[0, k, b] for k in range(slots_s.shape[1])]

    def write(b, at, attended):
        out_ref[b] = (
            block_at(hidden_s, at)
            + jnp.dot(jnp.concatenate(attended, 1).astype(BF16), outw_v[...], preferred_element_type=F32)
        ).astype(BF16)

    def far_inner(i, carry):
        b = i + 1
        after = jnp.minimum(b + 1, blocks - 2)
        at = pos_s[b]
        attended = []
        for group, (peak, total, den) in enumerate(attend(at, far_blocks(b), (pos_s[after], far_blocks(after)))):
            cols = slice(group * HALF, (group + 1) * HALF)
            peak, other = spread(peak), near_peak[i, :, cols]
            top = jnp.maximum(peak, other)
            mine, theirs = jnp.exp2((peak - top) * scale), jnp.exp2((other - top) * scale)
            attended.append(
                (spread(total) * mine + near_sum[i, :, cols] * theirs)
                / (spread(den) * mine + near_den[i, :, cols] * theirs)
            )
        write(b, at, attended)
        return carry

    score(pos_s[1], far_blocks(1), 0)
    lax.fori_loop(0, blocks - 2, far_inner, 0, unroll=2)

    for side, edge in zip(sides[:2], edges):
        pl.when(side[0])(edge.wait_send)
        pl.when(side[1])(edge.wait_recv)
    arrived = project(n_ctx, n_ctx + 2)
    for s, there, at, inner in (
        (n_ctx, ctx > 0, ctx * blocks - 1, 0),
        (n_ctx + 1, ctx < n_ctx - 1, (ctx + 1) * blocks, blocks - 1),
    ):
        valid = jnp.where(there, lens_s[0, jnp.where(there, at, 0)], 0)
        keep_far(s, arrived[(s - n_ctx) * BLK : (s - n_ctx + 1) * BLK], valid, block_at(key_s, pos_s[inner])[:1].astype(F32))

    def whole(i, carry):
        b = i * (blocks - 1)
        before = jnp.where(i == 0, left, pos_s[jnp.maximum(b - 1, 0)])
        after = jnp.where(i == 0, pos_s[jnp.minimum(b + 1, blocks - 1)], right)
        sources = [before, pos_s[b], after] + far_blocks(b)
        score(pos_s[b], sources, 0)
        results = attend(pos_s[b], sources, None)
        write(b, pos_s[b], [spread(total) / spread(den) for _, total, den in results])
        return carry

    lax.fori_loop(0, 2, whole, 0)


def on_device(
    feats,
    face_rows,
    neighbours,
    block_len,
    dilated,
    pick,
    cpe_weight,
    cpe_bias,
    ln_gain,
    ln_bias,
    w_qkv,
    w_out,
):
    n_space, n_ctx = lax.axis_size("space"), lax.axis_size("ctx")
    count = feats.shape[1]
    blocks = count // BLK
    kept = blocks + n_ctx + 2
    operands = (
        feats.reshape(blocks, BLK, D), face_rows, neighbours.transpose(2, 0, 1).reshape(OFFSETS, blocks, 1, BLK), block_len, dilated.transpose(0, 2, 1), pick,
        cpe_weight.reshape(-1, D), cpe_bias[None], ln_gain[None], ln_bias[None], w_qkv, w_out,
    )
    operands = [pltpu.with_memory_space_constraint(operand, pltpu.HBM) for operand in operands]
    shape = lambda i: operands[i].shape
    return pl.pallas_call(
        functools.partial(body, n_space, n_ctx),
        in_specs=[pl.BlockSpec(memory_space=pltpu.HBM)] * len(operands),
        out_specs=pl.BlockSpec(memory_space=pltpu.VMEM),
        out_shape=jax.ShapeDtypeStruct((blocks, BLK, D), BF16),
        scratch_shapes=[
            pltpu.VMEM(((count + 2 * EDGE + 3 * FACE) // BLK, BLK, D), BF16),
            pltpu.VMEM(shape(1), jnp.int32),
            pltpu.VMEM(shape(2), jnp.int32),
            pltpu.VMEM(shape(6), BF16),
            pltpu.VMEM(shape(7), F32),
            pltpu.VMEM(shape(8), F32),
            pltpu.VMEM(shape(9), F32),
            pltpu.VMEM(shape(10), BF16),
            pltpu.VMEM(shape(11), BF16),
            pltpu.SMEM(shape(3), jnp.int32),
            pltpu.SMEM(shape(4), jnp.int32),
            pltpu.SMEM(shape(5), jnp.int32),
            pltpu.SMEM((blocks,), jnp.int32),
            pltpu.SMEM((blocks,), jnp.int32),
            pltpu.VMEM((blocks, BLK, D), F32),
            pltpu.VMEM((blocks, BLK, D), BF16),
            pltpu.VMEM((blocks, BLK, D), BF16),
            pltpu.VMEM((kept, BLK, D), BF16),
            pltpu.VMEM((kept, BLK, D), BF16),
            pltpu.VMEM((kept, BLK, HALF), BF16),
            pltpu.VMEM((n_ctx, BLK, D), BF16),
            pltpu.VMEM((2, BLK, D), BF16),
            pltpu.VMEM((n_ctx + 2, BLK, D), BF16),
            pltpu.VMEM((blocks - 2, BLK, D), F32),
            pltpu.VMEM((blocks - 2, BLK, D), F32),
            pltpu.VMEM((blocks - 2, BLK, D), F32),
            pltpu.VMEM((blocks, OFFSETS * BLK, D), BF16),
            pltpu.VMEM((EARLY, OFFSETS * BLK, HALF), BF16),
            pltpu.VMEM((EARLY, OFFSETS * BLK, HALF), BF16),
            pltpu.VMEM((HALF * HEADS // D * BLK, 7 * BLK), F32),
            pltpu.VMEM((HALF * HEADS // D * BLK, 7 * BLK), F32),
            pltpu.SemaphoreType.DMA((len(operands),)),
            pltpu.SemaphoreType.DMA((4,)),
            pltpu.SemaphoreType.DMA((4,)),
            pltpu.SemaphoreType.DMA((n_ctx + 2,)),
            pltpu.SemaphoreType.DMA((n_ctx + 2,)),
        ],
        compiler_params=pltpu.CompilerParams(
            collective_id=0, has_side_effects=True, vmem_limit_bytes=48 * 2**20
        ),
    )(*operands).reshape(1, count, D)


def solution(mesh):
    placed = (
        P("space", "ctx", None),
        P("space", "ctx"),
        P("space", "ctx", None),
        P("space", None),
        P("space", "ctx", None),
        P("space", None, None),
        P(),
        P(),
        P(),
        P(),
        P(),
        P(),
    )
    return jax.shard_map(
        on_device, mesh=mesh, in_specs=placed, out_specs=P("space", "ctx", None), check_vma=False
    )
```

```python
import functools
import math

import jax
import jax.numpy as jnp
from jax import lax
from jax.experimental import pallas as pl
from jax.experimental.pallas import tpu as pltpu
from jax.sharding import PartitionSpec as P

D = 256
HEADS = 8
BLK = 128
EDGE = 128
FACE = 256
HALF = 128
OFFSETS = 6

MESH = pl.DeviceIdType.MESH
BF16 = jnp.bfloat16
F32 = jnp.float32

LOCAL_PARTS = tuple(range(1, 9)) + (12, 13)
SENT_PARTS = (0, 9, 10, 11, 14, 15)
EARLY = 6
GROUPS = (1, 4, 8)


def zero_like(value):
    return jnp.zeros_like(value)


def body(
    n_space, n_ctx,
    feats, face_rows, neighbours, block_len, dilated, pick, cpe_weight, cpe_bias, ln_gain, ln_bias, w_qkv, w_out,
    out_ref,
    table, rows_v, ids_v, weight_v, bias_v, gain_v, shift_v, qkv_v, outw_v,
    lens_s, slots_s, pick_s, pos_s, perm_s,
    hidden_s, query_s, normed_s, key_s, value_s, ones_s, outgoing, ends, far,
    near_peak, near_sum, near_den, picked_s, hot_s, high_s, scores_a, scores_b,
    load_sem, table_send, table_recv, send_sem, recv_sem,
):
    space, ctx = lax.axis_index("space"), lax.axis_index("ctx")
    blocks = feats.shape[0]
    count = blocks * BLK
    local = count + FACE

    scores_s = (scores_a, scores_b)
    barrier = pltpu.get_barrier_semaphore()

    def ctx_peer(j):
        turn = (j + 1) // 2
        return lax.rem(ctx + n_ctx // 2 + (n_ctx - turn if j % 2 else turn), n_ctx)

    for j in range(n_ctx - 1):
        pl.semaphore_signal(barrier, inc=1, device_id=(space, ctx_peer(j)), device_id_type=MESH)
    sides = (
        (ctx < n_ctx - 1, ctx > 0, (space, ctx + 1)),
        (ctx > 0, ctx < n_ctx - 1, (space, ctx - 1)),
        (space < n_space - 1, space > 0, (space + 1, ctx)),
        (space > 0, space < n_space - 1, (space - 1, ctx)),
    )
    for there, _, peer in sides[2:]:
        @pl.when(there)
        def _():
            pl.semaphore_signal(barrier, inc=1, device_id=peer, device_id_type=MESH)

    loads = [
        pltpu.make_async_copy(source, target, load_sem.at[i])
        for i, (source, target) in enumerate((
            (feats, table.at[pl.ds(0, blocks)]),
            (face_rows, rows_v),
            (pick, pick_s),
            (neighbours, ids_v),
            (block_len, lens_s),
            (dilated, slots_s),
            (cpe_weight, weight_v),
            (cpe_bias, bias_v),
            (ln_gain, gain_v),
            (ln_bias, shift_v),
            (w_qkv, qkv_v),
            (w_out, outw_v),
        ))
    ]
    for load in loads:
        load.start()

    lane = lax.broadcasted_iota(jnp.int32, (BLK, HALF), 1)
    row = lax.broadcasted_iota(jnp.int32, (BLK, 1), 0)

    def split_ids(columns):
        spread = jnp.concatenate([jnp.broadcast_to(ids, (BLK, BLK)).T for ids in columns], 0)
        lanes = lax.broadcasted_iota(jnp.int32, spread.shape, 1)
        hot = jnp.where((spread & (BLK - 1)) == lanes, 1.0, 0.0).astype(BF16)
        return hot, (spread >> 7).astype(F32).astype(BF16)

    def choose(hot, high, parts):
        return jnp.concatenate([jnp.where(high == BF16(part), hot, zero_like(hot)) for part in parts], 1)

    loads[2].wait()
    wanted = [pick_s[0, ctx, ctx_peer(j)] for j in range(n_ctx)]
    need = [jnp.int32(n_ctx + b) for b in range(blocks)]
    for j in reversed(range(n_ctx)):
        need = [jnp.where(wanted[j] == b, j, need[b]) for b in range(blocks)]
    position = [
        sum((need[a] < need[b]).astype(jnp.int32) for a in range(blocks) if a != b) for b in range(blocks)
    ]
    for b in range(blocks):
        pos_s[b] = position[b]
    for j in range(blocks):
        perm_s[j] = sum(jnp.where(position[b] == j, b, 0) for b in range(blocks))

    loads[0].wait()
    loads[1].wait()
    hot, high = split_ids([rows_v[:, i * BLK : (i + 1) * BLK] for i in range(FACE // BLK)])
    table[blocks : local // BLK] = jnp.dot(
        choose(hot, high, range(blocks)), table[:blocks].reshape(count, D), preferred_element_type=F32
    ).astype(BF16).reshape(FACE // BLK, BLK, D)

    pl.semaphore_wait(
        barrier, n_ctx - 1 + sides[2][0].astype(jnp.int32) + sides[3][0].astype(jnp.int32)
    )
    pieces = (
        (count - EDGE, local, EDGE),
        (0, local + EDGE, EDGE),
        (count, local + 2 * EDGE, FACE),
        (count, local + 2 * EDGE + FACE, FACE),
    )
    copies = [
        pltpu.make_async_remote_copy(
            src_ref=table.at[pl.ds(source // BLK, size // BLK)],
            dst_ref=table.at[pl.ds(target // BLK, size // BLK)],
            send_sem=table_send.at[i],
            recv_sem=table_recv.at[i],
            device_id=sides[i][2],
            device_id_type=MESH,
        )
        for i, (source, target, size) in enumerate(pieces)
    ]
    for i in (2, 3, 0, 1):
        pl.when(sides[i][0])(copies[i].start)
    for i, (_, target, size) in enumerate(pieces):
        @pl.when(jnp.logical_not(sides[i][1]))
        def _():
            table[target // BLK : (target + size) // BLK] = jnp.zeros((size // BLK, BLK, D), BF16)

    for load in loads[3:]:
        load.wait()

    def block_at(ref, index):
        return ref[index]

    def table_rows(first, last):
        return table[first // BLK : last // BLK].reshape(last - first, D)

    def step_ids(j):
        at = perm_s[j]
        return split_ids([ids_v[o, at] for o in range(OFFSETS)])

    def pick_early(j, carry):
        hot, high = hot_s[j], high_s[j] = step_ids(j)
        picked_s[j] = jnp.dot(
            choose(hot, high, LOCAL_PARTS), table_rows(0, local), preferred_element_type=F32
        ).astype(BF16)
        return carry

    lax.fori_loop(0, EARLY, pick_early, 0, unroll=2)

    for i in range(4):
        pl.when(sides[i][0])(copies[i].wait_send)
        pl.when(sides[i][1])(copies[i].wait_recv)

    def keep(index, keys, values, valid, spare):
        inside = row < valid
        key_s[index] = jnp.where(inside, keys, spare).astype(BF16)
        value_s[index] = jnp.where(inside, values, 0.0).astype(BF16)
        ones_s[index] = jnp.where(jnp.broadcast_to(inside, (BLK, HALF)), 1.0, 0.0).astype(BF16)

    def send(j):
        return pltpu.make_async_remote_copy(
            src_ref=outgoing.at[j],
            dst_ref=far.at[ctx],
            send_sem=send_sem.at[j],
            recv_sem=recv_sem.at[j],
            device_id=(space, ctx_peer(j)),
            device_id_type=MESH,
        )

    def start_send(j):
        outgoing[j] = block_at(normed_s, pos_s[pick_s[0, ctx, ctx_peer(j)]])
        send(j).start()

    def finish(first, last):
        steps = range(first, last)
        order = [perm_s[j] for j in steps]
        own = jnp.concatenate([table[block] for block in order], 0)
        taps = jnp.concatenate(
            [own]
            + [jnp.concatenate([picked_s[j, o * BLK : (o + 1) * BLK] for j in steps], 0) for o in range(OFFSETS)],
            1,
        )
        conv = jnp.dot(taps, weight_v[...], preferred_element_type=F32)
        hidden = own.astype(F32) + conv + bias_v[...]
        center = hidden - jnp.mean(hidden, axis=-1, keepdims=True)
        variance = jnp.mean(center * center, axis=-1, keepdims=True)
        normed = (center * lax.rsqrt(variance + 1e-05) * gain_v[...] + shift_v[...]).astype(BF16)
        for b, j in enumerate(steps):
            normed_s[j] = normed[b * BLK : (b + 1) * BLK]
        for j in steps:
            if j < n_ctx - 1:
                start_send(j)
        projected = jnp.dot(normed, qkv_v[...], preferred_element_type=F32)
        for b, j in enumerate(steps):
            part = slice(b * BLK, (b + 1) * BLK)
            hidden_s[j] = hidden[part]
            query_s[j] = projected[part, :D].astype(BF16)
            keys = projected[part, D : 2 * D]
            keep(j, keys, projected[part, 2 * D :], lens_s[0, ctx * blocks + order[b]], keys[:1])

    def pick_sent(j, carry):
        hot, high = hot_s[j], high_s[j]
        sent = jnp.dot(
            choose(hot, high, SENT_PARTS), table_rows(local, table.shape[0] * BLK), preferred_element_type=F32
        )
        picked_s[j] = (sent + picked_s[j].astype(F32)).astype(BF16)
        return carry

    def pick_late(j, carry):
        hot, high = step_ids(j)
        picked_s[j] = jnp.dot(
            choose(hot, high, LOCAL_PARTS + SENT_PARTS), table_rows(0, table.shape[0] * BLK),
            preferred_element_type=F32,
        ).astype(BF16)
        return carry

    first = 0
    for last in GROUPS:
        if first < EARLY:
            lax.fori_loop(first, min(last, EARLY), pick_sent, 0, unroll=True)
        if last > EARLY:
            lax.fori_loop(max(first, EARLY), last, pick_late, 0, unroll=2)
        finish(first, last)
        first = last

    ends[0] = block_at(normed_s, pos_s[0])
    ends[1] = block_at(normed_s, pos_s[blocks - 1])
    edges = [
        pltpu.make_async_remote_copy(
            src_ref=ends.at[source],
            dst_ref=far.at[slot],
            send_sem=send_sem.at[slot],
            recv_sem=recv_sem.at[slot],
            device_id=(space, peer),
            device_id_type=MESH,
        )
        for peer, source, slot in ((ctx + 1, 1, n_ctx), (ctx - 1, 0, n_ctx + 1))
    ]
    for side, edge in zip(sides[:2], edges):
        pl.when(side[0])(edge.start)
    for j in range(blocks, n_ctx - 1):
        start_send(j)
    far[ctx] = block_at(normed_s, pos_s[pick_s[0, ctx, ctx]])
    for i, side in enumerate(sides[:2]):
        @pl.when(jnp.logical_not(side[1]))
        def _():
            far[n_ctx + i] = jnp.zeros((BLK, D), BF16)

    head_dim = D // HEADS
    heads = HALF // head_dim
    head_of = lane // head_dim
    scale = math.log2(math.e) / math.sqrt(head_dim)
    groups = D // HALF

    def spread(stacked):
        result = None
        for head in range(heads):
            part = stacked[head * BLK : (head + 1) * BLK]
            part = jnp.broadcast_to(part, (BLK, HALF))
            result = part if result is None else jnp.where(head_of == head, part, result)
        return result

    def stack(ref, sources, group):
        cols = slice(group * HALF, (group + 1) * HALF)
        return jnp.concatenate([ref[index, :, cols] for index in sources], 0)

    def score(at, sources, group):
        part = query_s[at, :, group * HALF : (group + 1) * HALF]
        stacked = jnp.concatenate(
            [jnp.where(head_of == head, part, zero_like(part)) for head in range(heads)], 0
        )
        scores_s[group][:, : len(sources) * BLK] = lax.dot_general(
            stacked, stack(key_s, sources, group), (((1,), (1,)), ((), ())), preferred_element_type=F32
        )

    def weigh(sources, group):
        scores = scores_s[group][:, : len(sources) * BLK]
        peak = jnp.max(scores, axis=-1, keepdims=True)
        weights = jnp.exp2((scores - peak) * scale).astype(BF16)
        ones = jnp.concatenate([ones_s[index] for index in sources], 0)
        mixed = jnp.dot(
            weights, jnp.concatenate([stack(value_s, sources, group), ones], 1), preferred_element_type=F32
        )
        return peak, mixed[:, :HALF], mixed[:, HALF:]

    def attend(at, sources, then):
        score(at, sources, 1)
        first = weigh(sources, 0)
        if then is not None:
            score(*then, 0)
        return [first, weigh(sources, 1)]

    def near_blocks(b):
        return [pos_s[b - 1], pos_s[b], pos_s[b + 1]]

    def keep_near(i, results):
        for group, (peak, total, den) in enumerate(results):
            cols = slice(group * HALF, (group + 1) * HALF)
            near_peak[i, :, cols] = spread(peak)
            near_sum[i, :, cols] = spread(total)
            near_den[i, :, cols] = spread(den)

    def near(i, carry):
        b = i + 1
        after = jnp.minimum(b + 1, blocks - 2)
        keep_near(i, attend(pos_s[b], near_blocks(b), (pos_s[after], near_blocks(after))))
        return carry

    score(pos_s[1], near_blocks(1), 0)
    lax.fori_loop(0, blocks - 2, near, 0, unroll=3)
    for i, (b, own) in enumerate(((0, (0, 1)), (blocks - 1, (blocks - 2, blocks - 1)))):
        sources = [pos_s[c] for c in own]
        score(pos_s[b], sources, 0)
        keep_near(blocks - 2 + i, attend(pos_s[b], sources, None))

    for j in range(n_ctx - 1):
        send(j).wait()

    left, right = blocks + n_ctx, blocks + n_ctx + 1

    def project(first, last):
        return jnp.dot(
            far[first:last].reshape((last - first) * BLK, D), qkv_v[:, D:], preferred_element_type=F32
        )

    def keep_far(s, both, valid, spare):
        keys = both[:, :D]
        keep(blocks + s, keys, both[:, D:], valid, keys[:1] if spare is None else spare)

    arrived = project(0, n_ctx)

    for s in range(n_ctx):
        keep_far(s, arrived[s * BLK : (s + 1) * BLK], lens_s[0, s * blocks + pick_s[0, s, ctx]], None)
    def far_blocks(b):
        return [blocks + slots_s[0, k, b] for k in range(slots_s.shape[1])]

    def write(b, at, attended):
        out_ref[b] = (
            block_at(hidden_s, at)
            + jnp.dot(jnp.concatenate(attended, 1).astype(BF16), outw_v[...], preferred_element_type=F32)
        ).astype(BF16)

    def merge(b, i, results):
        attended = []
        for group, (peak, total, den) in enumerate(results):
            cols = slice(group * HALF, (group + 1) * HALF)
            peak, other = spread(peak), near_peak[i, :, cols]
            top = jnp.maximum(peak, other)
            mine, theirs = jnp.exp2((peak - top) * scale), jnp.exp2((other - top) * scale)
            attended.append(
                (spread(total) * mine + near_sum[i, :, cols] * theirs)
                / (spread(den) * mine + near_den[i, :, cols] * theirs)
            )
        write(b, pos_s[b], attended)

    def far_inner(i, carry):
        b = i + 1
        after = jnp.minimum(b + 1, blocks - 2)
        merge(b, i, attend(pos_s[b], far_blocks(b), (pos_s[after], far_blocks(after))))
        return carry

    score(pos_s[1], far_blocks(1), 0)
    lax.fori_loop(0, blocks - 2, far_inner, 0, unroll=3)

    for side, edge in zip(sides[:2], edges):
        pl.when(side[0])(edge.wait_send)
        pl.when(side[1])(edge.wait_recv)
    arrived = project(n_ctx, n_ctx + 2)
    for s, there, at, inner in (
        (n_ctx, ctx > 0, ctx * blocks - 1, 0),
        (n_ctx + 1, ctx < n_ctx - 1, (ctx + 1) * blocks, blocks - 1),
    ):
        valid = jnp.where(there, lens_s[0, jnp.where(there, at, 0)], 0)
        keep_far(s, arrived[(s - n_ctx) * BLK : (s - n_ctx + 1) * BLK], valid, block_at(key_s, pos_s[inner])[:1].astype(F32))

    for i, (b, end) in enumerate(((0, left), (blocks - 1, right))):
        sources = [end] + far_blocks(b)
        score(pos_s[b], sources, 0)
        merge(b, blocks - 2 + i, attend(pos_s[b], sources, None))


def on_device(
    feats,
    face_rows,
    neighbours,
    block_len,
    dilated,
    pick,
    cpe_weight,
    cpe_bias,
    ln_gain,
    ln_bias,
    w_qkv,
    w_out,
):
    n_space, n_ctx = lax.axis_size("space"), lax.axis_size("ctx")
    count = feats.shape[1]
    blocks = count // BLK
    kept = blocks + n_ctx + 2
    operands = (
        feats.reshape(blocks, BLK, D), face_rows, neighbours.transpose(2, 0, 1).reshape(OFFSETS, blocks, 1, BLK), block_len, dilated.transpose(0, 2, 1), pick,
        cpe_weight.reshape(-1, D), cpe_bias[None], ln_gain[None], ln_bias[None], w_qkv, w_out,
    )
    operands = [pltpu.with_memory_space_constraint(operand, pltpu.HBM) for operand in operands]
    shape = lambda i: operands[i].shape
    return pl.pallas_call(
        functools.partial(body, n_space, n_ctx),
        in_specs=[pl.BlockSpec(memory_space=pltpu.HBM)] * len(operands),
        out_specs=pl.BlockSpec(memory_space=pltpu.VMEM),
        out_shape=jax.ShapeDtypeStruct((blocks, BLK, D), BF16),
        scratch_shapes=[
            pltpu.VMEM(((count + 2 * EDGE + 3 * FACE) // BLK, BLK, D), BF16),
            pltpu.VMEM(shape(1), jnp.int32),
            pltpu.VMEM(shape(2), jnp.int32),
            pltpu.VMEM(shape(6), BF16),
            pltpu.VMEM(shape(7), F32),
            pltpu.VMEM(shape(8), F32),
            pltpu.VMEM(shape(9), F32),
            pltpu.VMEM(shape(10), BF16),
            pltpu.VMEM(shape(11), BF16),
            pltpu.SMEM(shape(3), jnp.int32),
            pltpu.SMEM(shape(4), jnp.int32),
            pltpu.SMEM(shape(5), jnp.int32),
            pltpu.SMEM((blocks,), jnp.int32),
            pltpu.SMEM((blocks,), jnp.int32),
            pltpu.VMEM((blocks, BLK, D), F32),
            pltpu.VMEM((blocks, BLK, D), BF16),
            pltpu.VMEM((blocks, BLK, D), BF16),
            pltpu.VMEM((kept, BLK, D), BF16),
            pltpu.VMEM((kept, BLK, D), BF16),
            pltpu.VMEM((kept, BLK, HALF), BF16),
            pltpu.VMEM((n_ctx, BLK, D), BF16),
            pltpu.VMEM((2, BLK, D), BF16),
            pltpu.VMEM((n_ctx + 2, BLK, D), BF16),
            pltpu.VMEM((blocks, BLK, D), F32),
            pltpu.VMEM((blocks, BLK, D), F32),
            pltpu.VMEM((blocks, BLK, D), F32),
            pltpu.VMEM((blocks, OFFSETS * BLK, D), BF16),
            pltpu.VMEM((EARLY, OFFSETS * BLK, HALF), BF16),
            pltpu.VMEM((EARLY, OFFSETS * BLK, HALF), BF16),
            pltpu.VMEM((HALF * HEADS // D * BLK, 7 * BLK), F32),
            pltpu.VMEM((HALF * HEADS // D * BLK, 7 * BLK), F32),
            pltpu.SemaphoreType.DMA((len(operands),)),
            pltpu.SemaphoreType.DMA((4,)),
            pltpu.SemaphoreType.DMA((4,)),
            pltpu.SemaphoreType.DMA((n_ctx + 2,)),
            pltpu.SemaphoreType.DMA((n_ctx + 2,)),
        ],
        compiler_params=pltpu.CompilerParams(
            collective_id=0, has_side_effects=True, vmem_limit_bytes=48 * 2**20
        ),
    )(*operands).reshape(1, count, D)


def solution(mesh):
    placed = (
        P("space", "ctx", None),
        P("space", "ctx"),
        P("space", "ctx", None),
        P("space", None),
        P("space", "ctx", None),
        P("space", None, None),
        P(),
        P(),
        P(),
        P(),
        P(),
        P(),
    )
    return jax.shard_map(
        on_device, mesh=mesh, in_specs=placed, out_specs=P("space", "ctx", None), check_vma=False
    )
```

```python
import functools
import math

import jax
import jax.numpy as jnp
from jax import lax
from jax.experimental import pallas as pl
from jax.experimental.pallas import tpu as pltpu
from jax.sharding import PartitionSpec as P

D = 256
HEADS = 8
BLK = 128
EDGE = 128
FACE = 256
HALF = 128
OFFSETS = 6

MESH = pl.DeviceIdType.MESH
BF16 = jnp.bfloat16
F32 = jnp.float32

LOCAL_PARTS = tuple(range(1, 9)) + (12, 13)
SENT_PARTS = (0, 9, 10, 11, 14, 15)
EARLY = 6
GROUPS = (1, 4, 8)


def zero_like(value):
    return jnp.zeros_like(value)


def body(
    n_space, n_ctx,
    feats, face_rows, neighbours, block_len, dilated, pick, cpe_weight, cpe_bias, ln_gain, ln_bias, w_qkv, w_out,
    out_ref,
    table, rows_v, ids_v, weight_v, bias_v, gain_v, shift_v, qkv_v, outw_v,
    lens_s, slots_s, pick_s, pos_s, perm_s,
    hidden_s, query_s, normed_s, key_s, value_s, ones_s, outgoing, ends, far,
    near_peak, near_sum, near_den, picked_s, hot_s, high_s, scores_a, scores_b,
    load_sem, table_send, table_recv, send_sem, recv_sem,
):
    space, ctx = lax.axis_index("space"), lax.axis_index("ctx")
    blocks = feats.shape[0]
    count = blocks * BLK
    local = count + FACE

    scores_s = (scores_a, scores_b)
    barrier = pltpu.get_barrier_semaphore()

    def ctx_peer(j):
        turn = (j + 1) // 2
        return lax.rem(ctx + n_ctx // 2 + (n_ctx - turn if j % 2 else turn), n_ctx)

    for j in range(n_ctx - 1):
        pl.semaphore_signal(barrier, inc=1, device_id=(space, ctx_peer(j)), device_id_type=MESH)
    sides = (
        (ctx < n_ctx - 1, ctx > 0, (space, ctx + 1)),
        (ctx > 0, ctx < n_ctx - 1, (space, ctx - 1)),
        (space < n_space - 1, space > 0, (space + 1, ctx)),
        (space > 0, space < n_space - 1, (space - 1, ctx)),
    )
    for there, _, peer in sides[2:]:
        @pl.when(there)
        def _():
            pl.semaphore_signal(barrier, inc=1, device_id=peer, device_id_type=MESH)

    loads = [
        pltpu.make_async_copy(source, target, load_sem.at[i])
        for i, (source, target) in enumerate((
            (feats, table.at[pl.ds(0, blocks)]),
            (face_rows, rows_v),
            (pick, pick_s),
            (neighbours, ids_v),
            (block_len, lens_s),
            (dilated, slots_s),
            (cpe_weight, weight_v),
            (cpe_bias, bias_v),
            (ln_gain, gain_v),
            (ln_bias, shift_v),
            (w_qkv, qkv_v),
            (w_out, outw_v),
        ))
    ]
    for load in loads:
        load.start()

    lane = lax.broadcasted_iota(jnp.int32, (BLK, HALF), 1)
    row = lax.broadcasted_iota(jnp.int32, (BLK, 1), 0)

    def split_ids(columns):
        spread = jnp.concatenate([jnp.broadcast_to(ids, (BLK, BLK)).T for ids in columns], 0)
        lanes = lax.broadcasted_iota(jnp.int32, spread.shape, 1)
        hot = jnp.where((spread & (BLK - 1)) == lanes, 1.0, 0.0).astype(BF16)
        return hot, (spread >> 7).astype(F32).astype(BF16)

    def choose(hot, high, parts):
        return jnp.concatenate([jnp.where(high == BF16(part), hot, zero_like(hot)) for part in parts], 1)

    loads[2].wait()
    wanted = [pick_s[0, ctx, ctx_peer(j)] for j in range(n_ctx)]
    need = [jnp.int32(n_ctx + b) for b in range(blocks)]
    for j in reversed(range(n_ctx)):
        need = [jnp.where(wanted[j] == b, j, need[b]) for b in range(blocks)]
    position = [
        sum((need[a] < need[b]).astype(jnp.int32) for a in range(blocks) if a != b) for b in range(blocks)
    ]
    for b in range(blocks):
        pos_s[b] = position[b]
    for j in range(blocks):
        perm_s[j] = sum(jnp.where(position[b] == j, b, 0) for b in range(blocks))

    loads[0].wait()
    loads[1].wait()
    hot, high = split_ids([rows_v[:, i * BLK : (i + 1) * BLK] for i in range(FACE // BLK)])
    table[blocks : local // BLK] = jnp.dot(
        choose(hot, high, range(blocks)), table[:blocks].reshape(count, D), preferred_element_type=F32
    ).astype(BF16).reshape(FACE // BLK, BLK, D)

    pl.semaphore_wait(
        barrier, n_ctx - 1 + sides[2][0].astype(jnp.int32) + sides[3][0].astype(jnp.int32)
    )
    pieces = (
        (count - EDGE, local, EDGE),
        (0, local + EDGE, EDGE),
        (count, local + 2 * EDGE, FACE),
        (count, local + 2 * EDGE + FACE, FACE),
    )
    copies = [
        pltpu.make_async_remote_copy(
            src_ref=table.at[pl.ds(source // BLK, size // BLK)],
            dst_ref=table.at[pl.ds(target // BLK, size // BLK)],
            send_sem=table_send.at[i],
            recv_sem=table_recv.at[i],
            device_id=sides[i][2],
            device_id_type=MESH,
        )
        for i, (source, target, size) in enumerate(pieces)
    ]
    for i in (2, 3, 0, 1):
        pl.when(sides[i][0])(copies[i].start)
    for i, (_, target, size) in enumerate(pieces):
        @pl.when(jnp.logical_not(sides[i][1]))
        def _():
            table[target // BLK : (target + size) // BLK] = jnp.zeros((size // BLK, BLK, D), BF16)

    for load in loads[3:]:
        load.wait()

    def block_at(ref, index):
        return ref[index]

    def table_rows(first, last):
        return table[first // BLK : last // BLK].reshape(last - first, D)

    def step_ids(j):
        at = perm_s[j]
        return split_ids([ids_v[o, at] for o in range(OFFSETS)])

    def pick_early(j, carry):
        hot, high = hot_s[j], high_s[j] = step_ids(j)
        picked_s[j] = jnp.dot(
            choose(hot, high, LOCAL_PARTS), table_rows(0, local), preferred_element_type=F32
        ).astype(BF16)
        return carry

    lax.fori_loop(0, EARLY, pick_early, 0, unroll=2)

    for i in range(4):
        pl.when(sides[i][0])(copies[i].wait_send)
        pl.when(sides[i][1])(copies[i].wait_recv)

    def keep(index, keys, values, valid, spare):
        inside = row < valid
        key_s[index] = jnp.where(inside, keys, spare).astype(BF16)
        value_s[index] = jnp.where(inside, values, 0.0).astype(BF16)
        ones_s[index] = jnp.where(jnp.broadcast_to(inside, (BLK, HALF)), 1.0, 0.0).astype(BF16)

    def send(j):
        return pltpu.make_async_remote_copy(
            src_ref=outgoing.at[j],
            dst_ref=far.at[ctx],
            send_sem=send_sem.at[j],
            recv_sem=recv_sem.at[j],
            device_id=(space, ctx_peer(j)),
            device_id_type=MESH,
        )

    def start_send(j):
        outgoing[j] = block_at(normed_s, pos_s[pick_s[0, ctx, ctx_peer(j)]])
        send(j).start()

    def finish(first, last):
        steps = range(first, last)
        order = [perm_s[j] for j in steps]
        own = jnp.concatenate([table[block] for block in order], 0)
        taps = jnp.concatenate(
            [own]
            + [jnp.concatenate([picked_s[j, o * BLK : (o + 1) * BLK] for j in steps], 0) for o in range(OFFSETS)],
            1,
        )
        conv = jnp.dot(taps, weight_v[...], preferred_element_type=F32)
        hidden = own.astype(F32) + conv + bias_v[...]
        center = hidden - jnp.mean(hidden, axis=-1, keepdims=True)
        variance = jnp.mean(center * center, axis=-1, keepdims=True)
        normed = (center * lax.rsqrt(variance + 1e-05) * gain_v[...] + shift_v[...]).astype(BF16)
        for b, j in enumerate(steps):
            normed_s[j] = normed[b * BLK : (b + 1) * BLK]
        for j in steps:
            if j < n_ctx - 1:
                start_send(j)
        projected = jnp.dot(normed, qkv_v[...], preferred_element_type=F32)
        for b, j in enumerate(steps):
            part = slice(b * BLK, (b + 1) * BLK)
            hidden_s[j] = hidden[part]
            query_s[j] = projected[part, :D].astype(BF16)
            keys = projected[part, D : 2 * D]
            keep(j, keys, projected[part, 2 * D :], lens_s[0, ctx * blocks + order[b]], keys[:1])

    def pick_sent(j, carry):
        hot, high = hot_s[j], high_s[j]
        sent = jnp.dot(
            choose(hot, high, SENT_PARTS), table_rows(local, table.shape[0] * BLK), preferred_element_type=F32
        )
        picked_s[j] = (sent + picked_s[j].astype(F32)).astype(BF16)
        return carry

    def pick_late(j, carry):
        hot, high = step_ids(j)
        picked_s[j] = jnp.dot(
            choose(hot, high, LOCAL_PARTS + SENT_PARTS), table_rows(0, table.shape[0] * BLK),
            preferred_element_type=F32,
        ).astype(BF16)
        return carry

    first = 0
    for last in GROUPS:
        if first < EARLY:
            lax.fori_loop(first, min(last, EARLY), pick_sent, 0, unroll=True)
        if last > EARLY:
            lax.fori_loop(max(first, EARLY), last, pick_late, 0, unroll=2)
        finish(first, last)
        first = last

    ends[0] = block_at(normed_s, pos_s[0])
    ends[1] = block_at(normed_s, pos_s[blocks - 1])
    edges = [
        pltpu.make_async_remote_copy(
            src_ref=ends.at[source],
            dst_ref=far.at[slot],
            send_sem=send_sem.at[slot],
            recv_sem=recv_sem.at[slot],
            device_id=(space, peer),
            device_id_type=MESH,
        )
        for peer, source, slot in ((ctx + 1, 1, n_ctx), (ctx - 1, 0, n_ctx + 1))
    ]
    for side, edge in zip(sides[:2], edges):
        pl.when(side[0])(edge.start)
    for j in range(blocks, n_ctx - 1):
        start_send(j)
    far[ctx] = block_at(normed_s, pos_s[pick_s[0, ctx, ctx]])
    for i, side in enumerate(sides[:2]):
        @pl.when(jnp.logical_not(side[1]))
        def _():
            far[n_ctx + i] = jnp.zeros((BLK, D), BF16)

    head_dim = D // HEADS
    heads = HALF // head_dim
    head_of = lane // head_dim
    scale = math.log2(math.e) / math.sqrt(head_dim)
    groups = D // HALF

    def spread(stacked):
        result = None
        for head in range(heads):
            part = stacked[head * BLK : (head + 1) * BLK]
            part = jnp.broadcast_to(part, (BLK, HALF))
            result = part if result is None else jnp.where(head_of == head, part, result)
        return result

    def stack(ref, sources, group):
        cols = slice(group * HALF, (group + 1) * HALF)
        return jnp.concatenate([ref[index, :, cols] for index in sources], 0)

    def score(at, sources, group):
        part = query_s[at, :, group * HALF : (group + 1) * HALF]
        stacked = jnp.concatenate(
            [jnp.where(head_of == head, part, zero_like(part)) for head in range(heads)], 0
        )
        scores_s[group][:, : len(sources) * BLK] = lax.dot_general(
            stacked, stack(key_s, sources, group), (((1,), (1,)), ((), ())), preferred_element_type=F32
        )

    def weigh(sources, group):
        scores = scores_s[group][:, : len(sources) * BLK]
        peak = jnp.max(scores, axis=-1, keepdims=True)
        weights = jnp.exp2((scores - peak) * scale).astype(BF16)
        ones = jnp.concatenate([ones_s[index] for index in sources], 0)
        mixed = jnp.dot(
            weights, jnp.concatenate([stack(value_s, sources, group), ones], 1), preferred_element_type=F32
        )
        return peak, mixed[:, :HALF], mixed[:, HALF:]

    def attend(at, sources, then):
        score(at, sources, 1)
        first = weigh(sources, 0)
        if then is not None:
            score(*then, 0)
        return [first, weigh(sources, 1)]

    def near_blocks(b):
        return [pos_s[b - 1], pos_s[b], pos_s[b + 1]]

    def keep_near(i, results):
        for group, (peak, total, den) in enumerate(results):
            cols = slice(group * HALF, (group + 1) * HALF)
            near_peak[i, :, cols] = spread(peak)
            near_sum[i, :, cols] = spread(total)
            near_den[i, :, cols] = spread(den)

    def near(i, carry):
        b = i + 1
        after = jnp.minimum(b + 1, blocks - 2)
        keep_near(i, attend(pos_s[b], near_blocks(b), (pos_s[after], near_blocks(after))))
        return carry

    score(pos_s[1], near_blocks(1), 0)
    lax.fori_loop(0, blocks - 2, near, 0, unroll=3)
    for i, (b, own) in enumerate(((0, (0, 1)), (blocks - 1, (blocks - 2, blocks - 1)))):
        sources = [pos_s[c] for c in own]
        score(pos_s[b], sources, 0)
        keep_near(blocks - 2 + i, attend(pos_s[b], sources, None))

    for j in range(n_ctx - 1):
        send(j).wait()

    left, right = blocks + n_ctx, blocks + n_ctx + 1

    def project(first, last):
        return jnp.dot(
            far[first:last].reshape((last - first) * BLK, D), qkv_v[:, D:], preferred_element_type=F32
        )

    def keep_far(s, both, valid, spare):
        keys = both[:, :D]
        keep(blocks + s, keys, both[:, D:], valid, keys[:1] if spare is None else spare)

    arrived = project(0, n_ctx)

    for s in range(n_ctx):
        keep_far(s, arrived[s * BLK : (s + 1) * BLK], lens_s[0, s * blocks + pick_s[0, s, ctx]], None)
    def far_blocks(b):
        return [blocks + slots_s[0, k, b] for k in range(slots_s.shape[1])]

    def write(b, at, attended):
        out_ref[b] = (
            block_at(hidden_s, at)
            + jnp.dot(jnp.concatenate(attended, 1).astype(BF16), outw_v[...], preferred_element_type=F32)
        ).astype(BF16)

    def merge(b, i, results):
        attended = []
        for group, (peak, total, den) in enumerate(results):
            cols = slice(group * HALF, (group + 1) * HALF)
            peak, other = spread(peak), near_peak[i, :, cols]
            top = jnp.maximum(peak, other)
            mine, theirs = jnp.exp2((peak - top) * scale), jnp.exp2((other - top) * scale)
            attended.append(
                (spread(total) * mine + near_sum[i, :, cols] * theirs)
                / (spread(den) * mine + near_den[i, :, cols] * theirs)
            )
        write(b, pos_s[b], attended)

    def far_inner(i, carry):
        b = i + 1
        after = jnp.minimum(b + 1, blocks - 2)
        merge(b, i, attend(pos_s[b], far_blocks(b), (pos_s[after], far_blocks(after))))
        return carry

    score(pos_s[1], far_blocks(1), 0)
    lax.fori_loop(0, blocks - 2, far_inner, 0, unroll=True)

    for side, edge in zip(sides[:2], edges):
        pl.when(side[0])(edge.wait_send)
        pl.when(side[1])(edge.wait_recv)
    arrived = project(n_ctx, n_ctx + 2)
    for s, there, at, inner in (
        (n_ctx, ctx > 0, ctx * blocks - 1, 0),
        (n_ctx + 1, ctx < n_ctx - 1, (ctx + 1) * blocks, blocks - 1),
    ):
        valid = jnp.where(there, lens_s[0, jnp.where(there, at, 0)], 0)
        keep_far(s, arrived[(s - n_ctx) * BLK : (s - n_ctx + 1) * BLK], valid, block_at(key_s, pos_s[inner])[:1].astype(F32))

    for i, (b, end) in enumerate(((0, left), (blocks - 1, right))):
        sources = [end] + far_blocks(b)
        score(pos_s[b], sources, 0)
        merge(b, blocks - 2 + i, attend(pos_s[b], sources, None))


def on_device(
    feats,
    face_rows,
    neighbours,
    block_len,
    dilated,
    pick,
    cpe_weight,
    cpe_bias,
    ln_gain,
    ln_bias,
    w_qkv,
    w_out,
):
    n_space, n_ctx = lax.axis_size("space"), lax.axis_size("ctx")
    count = feats.shape[1]
    blocks = count // BLK
    kept = blocks + n_ctx + 2
    operands = (
        feats.reshape(blocks, BLK, D), face_rows, neighbours.transpose(2, 0, 1).reshape(OFFSETS, blocks, 1, BLK), block_len, dilated.transpose(0, 2, 1), pick,
        cpe_weight.reshape(-1, D), cpe_bias[None], ln_gain[None], ln_bias[None], w_qkv, w_out,
    )
    operands = [pltpu.with_memory_space_constraint(operand, pltpu.HBM) for operand in operands]
    shape = lambda i: operands[i].shape
    return pl.pallas_call(
        functools.partial(body, n_space, n_ctx),
        in_specs=[pl.BlockSpec(memory_space=pltpu.HBM)] * len(operands),
        out_specs=pl.BlockSpec(memory_space=pltpu.VMEM),
        out_shape=jax.ShapeDtypeStruct((blocks, BLK, D), BF16),
        scratch_shapes=[
            pltpu.VMEM(((count + 2 * EDGE + 3 * FACE) // BLK, BLK, D), BF16),
            pltpu.VMEM(shape(1), jnp.int32),
            pltpu.VMEM(shape(2), jnp.int32),
            pltpu.VMEM(shape(6), BF16),
            pltpu.VMEM(shape(7), F32),
            pltpu.VMEM(shape(8), F32),
            pltpu.VMEM(shape(9), F32),
            pltpu.VMEM(shape(10), BF16),
            pltpu.VMEM(shape(11), BF16),
            pltpu.SMEM(shape(3), jnp.int32),
            pltpu.SMEM(shape(4), jnp.int32),
            pltpu.SMEM(shape(5), jnp.int32),
            pltpu.SMEM((blocks,), jnp.int32),
            pltpu.SMEM((blocks,), jnp.int32),
            pltpu.VMEM((blocks, BLK, D), F32),
            pltpu.VMEM((blocks, BLK, D), BF16),
            pltpu.VMEM((blocks, BLK, D), BF16),
            pltpu.VMEM((kept, BLK, D), BF16),
            pltpu.VMEM((kept, BLK, D), BF16),
            pltpu.VMEM((kept, BLK, HALF), BF16),
            pltpu.VMEM((n_ctx, BLK, D), BF16),
            pltpu.VMEM((2, BLK, D), BF16),
            pltpu.VMEM((n_ctx + 2, BLK, D), BF16),
            pltpu.VMEM((blocks, BLK, D), F32),
            pltpu.VMEM((blocks, BLK, D), F32),
            pltpu.VMEM((blocks, BLK, D), F32),
            pltpu.VMEM((blocks, OFFSETS * BLK, D), BF16),
            pltpu.VMEM((EARLY, OFFSETS * BLK, HALF), BF16),
            pltpu.VMEM((EARLY, OFFSETS * BLK, HALF), BF16),
            pltpu.VMEM((HALF * HEADS // D * BLK, 7 * BLK), F32),
            pltpu.VMEM((HALF * HEADS // D * BLK, 7 * BLK), F32),
            pltpu.SemaphoreType.DMA((len(operands),)),
            pltpu.SemaphoreType.DMA((4,)),
            pltpu.SemaphoreType.DMA((4,)),
            pltpu.SemaphoreType.DMA((n_ctx + 2,)),
            pltpu.SemaphoreType.DMA((n_ctx + 2,)),
        ],
        compiler_params=pltpu.CompilerParams(
            collective_id=0, has_side_effects=True, vmem_limit_bytes=48 * 2**20
        ),
    )(*operands).reshape(1, count, D)


def solution(mesh):
    placed = (
        P("space", "ctx", None),
        P("space", "ctx"),
        P("space", "ctx", None),
        P("space", None),
        P("space", "ctx", None),
        P("space", None, None),
        P(),
        P(),
        P(),
        P(),
        P(),
        P(),
    )
    return jax.shard_map(
        on_device, mesh=mesh, in_specs=placed, out_specs=P("space", "ctx", None), check_vma=False
    )
```
